256 devices in a mesh: ap: 32 (over z, y_hi, core), tm: 8 (over x, y_lo).
Axes of the slice: x: 4, y: 4 (y_hi: 2, y_lo: 2; y = y_hi * 2 + y_lo), z: 8, core: 2. Of those that a mesh axis runs over, the one named last changes fastest.
Arguments:
- voltages: bfloat16 [128, 64, 128, 256], P('tm', None, 'ap'), may hold values from -6 to 6
Outputs:
- visibility: float32 [256, 2, 64, 256], P('tm', None, 'ap')
The draws below stay inside these ranges and needn't reach their ends.
All inputs are finite; a program needn't handle non-finite values.
Results may differ from the reference program's by a relative error of at most 0.012.
Values may be sent and summed in bfloat16 or wider, within the bound.
No kernel may reach another device: no remote copies, remote signals or barrier semaphores. Data moves between devices by JAX's collectives and lax.ppermute only.
A program may use at most 128 MiB of HBM per device.

```python
import math
import jax
import jax.numpy as jnp
from jax import lax

G = 128
CH = 64
TIME = 128


def levels(rng, extent, cuts, least, top_value):
    gain, own = 1.0, jax.random.fold_in(rng, 6)
    for position, parts in cuts:
        steps = jnp.exp(jax.random.uniform(jax.random.fold_in(own, position), (parts,), jnp.float32, least / len(cuts), top_value / len(cuts)))
        gain = gain * jnp.repeat(steps, extent[position] // parts).reshape([-1 if axis == position else 1 for axis in range(len(extent))])
    return gain


def gaussian(rng, shape, spread, reach, cuts=(), kind=jnp.bfloat16):
    factor_of = levels(rng, shape, cuts, -0.22, 0.18) if cuts else 1.0
    drawn = jax.random.normal(rng, shape, jnp.float32) * spread * factor_of
    return jnp.minimum(jnp.maximum(drawn, -reach), reach).astype(kind)


def setup_inputs(seed: int = 0) -> dict:
    key_list = jax.random.split(jax.random.key(seed), 2)
    voltages = gaussian(key_list[0], (TIME, CH, G, 2 * G), 1.0, 6.0, ((0, 8), (2, 32)))
    return {"voltages": voltages}


two_pi = 2.0 * math.pi

def column_table(grid_side, pad_side):
    dishes = jnp.arange(grid_side, dtype=jnp.int32)
    columns = jnp.arange(pad_side, dtype=jnp.int32)
    angle = (dishes[:, None] * columns[None, :] % pad_side).astype(jnp.float32) * (two_pi / pad_side)
    cosine = jnp.cos(angle)
    sine = jnp.sin(angle)
    upper = jnp.concatenate([cosine, -sine], axis=1)
    lower = jnp.concatenate([sine, cosine], axis=1)
    return jnp.concatenate([upper, lower], axis=0).astype(jnp.bfloat16)

def row_table(grid_side, pad_side):
    beams = jnp.arange(pad_side, dtype=jnp.int32)
    dishes = jnp.arange(grid_side, dtype=jnp.int32)
    angle = (beams[:, None] * dishes[None, :] % pad_side).astype(jnp.float32) * (two_pi / pad_side)
    return jnp.concatenate([jnp.cos(angle), jnp.sin(angle)], axis=0).astype(jnp.bfloat16)

def lag_table(pad_side):
    index = jnp.arange(pad_side, dtype=jnp.int32)
    angle = (index[:, None] * index[None, :] % pad_side).astype(jnp.float32) * (two_pi / pad_side)
    return jnp.concatenate([jnp.cos(angle), jnp.sin(angle)], axis=1)

def power_of(mixed, pad_side):
    beam_real = mixed[..., :pad_side, :pad_side] + mixed[..., pad_side:, pad_side:]
    beam_imag = mixed[..., :pad_side, pad_side:] - mixed[..., pad_side:, :pad_side]
    return beam_real * beam_real + beam_imag * beam_imag

def finish(raw, lag_rows, grid_side, pad_side, samples):
    lag_cols = jnp.arange(pad_side, dtype=jnp.int32)
    signed_rows = jnp.where(lag_rows < grid_side, lag_rows, lag_rows - pad_side)
    signed_cols = jnp.where(lag_cols < grid_side, lag_cols, lag_cols - pad_side)
    pairs_rows = jnp.maximum(grid_side - jnp.abs(signed_rows), 0)
    pairs_cols = jnp.maximum(grid_side - jnp.abs(signed_cols), 0)
    count = pairs_rows[:, None] * pairs_cols[None, :]
    keep = (count > 0) & jnp.logical_not((lag_rows[:, None] == 0) & (lag_cols[None, :] == 0))
    denom = float(pad_side * pad_side) * jnp.sqrt(jnp.maximum(count, 1).astype(jnp.float32) * float(samples))
    factor = jnp.where(keep, 1.0 / denom, 0.0)
    return raw * factor[:, None, None, :]

def reference(voltages):
    samples, channels, grid_side, twice = voltages.shape
    pad_side = 2 * grid_side
    first = column_table(grid_side, pad_side)
    second = row_table(grid_side, pad_side).astype(jnp.float32)

    def one_sample(total, sample):
        field = jnp.dot(sample.reshape(channels * grid_side, twice), first, preferred_element_type=jnp.float32)
        field = field.astype(jnp.bfloat16).reshape(channels, grid_side, 2 * pad_side)
        mixed = jnp.einsum('wr,crk->cwk', second, field.astype(jnp.float32))
        return (total + power_of(mixed, pad_side), None)
    start = jnp.zeros((channels, pad_side, pad_side), jnp.float32)
    power, unused = lax.scan(one_sample, start, voltages)
    table = lag_table(pad_side)
    half = jnp.einsum('cuk,kj->cuj', power, table, precision=lax.Precision.HIGHEST)
    cosine = table[:, :pad_side]
    sine = table[:, pad_side:]
    first_sum = jnp.einsum('lu,cuj->lcj', cosine, half, precision=lax.Precision.HIGHEST)
    second_sum = jnp.einsum('lu,cuj->lcj', sine, half, precision=lax.Precision.HIGHEST)
    vis_real = first_sum[..., :pad_side] - second_sum[..., pad_side:]
    vis_imag = first_sum[..., pad_side:] + second_sum[..., :pad_side]
    raw = jnp.stack([vis_real, vis_imag], axis=1)
    lag_rows = jnp.arange(pad_side, dtype=jnp.int32)
    return finish(raw, lag_rows, grid_side, pad_side, samples)
```

```python
import functools
import math

import jax
import jax.numpy as jnp
import numpy as np
from jax import lax
from jax.experimental import pallas as pl
from jax.experimental.pallas import tpu as pltpu
from jax.sharding import PartitionSpec as P

F32 = jnp.float32
BF16 = jnp.bfloat16


def angles(rows, cols, pad_side):
    return (rows[:, None] * cols[None, :] % pad_side) * (2.0 * math.pi / pad_side)


def split(table):
    high = table.astype(BF16)
    low = (table - high.astype(np.float32)).astype(BF16)
    return high, low


def tables(grid_side, pad_side, samples):
    dishes, index = np.arange(grid_side), np.arange(pad_side)
    columns = angles(dishes, index, pad_side)
    cosine, sine = np.cos(columns), np.sin(columns)
    first = np.concatenate(
        [np.concatenate([cosine, -sine], 1), np.concatenate([sine, cosine], 1)], 0
    ).astype(BF16)
    second = np.concatenate([cosine.T, sine.T], 1).astype(BF16)
    whole = angles(index, index, pad_side)
    lag = np.concatenate([np.cos(whole), np.sin(whole)], 1).astype(np.float32)
    signed = np.where(index < grid_side, index, index - pad_side)
    pairs = np.maximum(grid_side - np.abs(signed), 0)
    count = pairs[:, None] * pairs[None, :]
    keep = (count > 0) & ((index[:, None] > 0) | (index[None, :] > 0))
    scale = 1.0 / (float(pad_side * pad_side) * np.sqrt(np.maximum(count, 1) * float(samples)))
    factor = np.where(keep, scale, 0.0).astype(np.float32)
    return first, second, *split(lag), factor


def dot(a, b):
    return jnp.dot(a, b, preferred_element_type=F32)


def halves(value):
    high = value.astype(BF16)
    return high, (value - high.astype(F32)).astype(BF16)


def dot3(a, b):
    return dot(a[0], b[0]) + (dot(a[0], b[1]) + dot(a[1], b[0]))


def correlate(v_ref, first_ref, second_ref, lag_hi_ref, lag_lo_ref, factor_ref, out_ref, power_ref):
    samples, channels = v_ref.shape[:2]
    pad = second_ref.shape[0]
    owned = out_ref.shape[3]
    power_ref[...] = jnp.zeros_like(power_ref)

    def sample(t, carry):
        for c in range(channels):
            field = dot(v_ref[t, c], first_ref[...]).astype(BF16)
            real, imag = field[:, :pad], field[:, pad:]
            stacked = jnp.concatenate(
                [jnp.concatenate([real, imag], 1), jnp.concatenate([imag, -real], 1)], 0
            )
            beam = dot(second_ref[...], stacked)
            power_ref[c] += beam[:, :pad] * beam[:, :pad] + beam[:, pad:] * beam[:, pad:]
        return carry

    lax.fori_loop(0, samples, sample, 0)
    lag = (lag_hi_ref[...], lag_lo_ref[...])
    for c in range(channels):
        half = dot3(halves(power_ref[c]), lag)
        real, imag = half[:, :pad], half[:, pad:]
        stacked = jnp.concatenate(
            [jnp.concatenate([real, imag], 1), jnp.concatenate([-imag, real], 1)], 0
        )
        raw = dot3(lag, halves(stacked))
        for part in range(2):
            terms = (raw[:, part * pad : (part + 1) * pad] * factor_ref[...]).astype(BF16)
            out_ref[:, part, c] = terms.reshape(pad // owned, owned, pad)


def shards(voltages):
    samples, channels, local_rows, twice = voltages.shape
    grid_side = twice // 2
    pad_side = 2 * grid_side
    over_ap, over_tm = lax.axis_size("ap"), lax.axis_size("tm")
    own = channels // over_ap
    owned = pad_side // over_tm
    consts = tables(grid_side, pad_side, samples * over_tm)
    sent = voltages.reshape(samples, over_ap, own, local_rows, twice).transpose(1, 0, 2, 3, 4)
    got = lax.all_to_all(sent, "ap", 0, 0, tiled=True)
    rows = got.transpose(1, 2, 0, 3, 4).reshape(samples, own, grid_side, twice)
    terms = pl.pallas_call(
        correlate,
        out_shape=jax.ShapeDtypeStruct((over_tm, 2, own, owned, pad_side), BF16),
        in_specs=[pl.BlockSpec(memory_space=pltpu.VMEM)] * 6,
        out_specs=pl.BlockSpec(memory_space=pltpu.VMEM),
        scratch_shapes=[pltpu.VMEM((own, pad_side, pad_side), F32)],
        compiler_params=pltpu.CompilerParams(vmem_limit_bytes=40 * 1024 * 1024),
        name="correlate",
    )(rows, *[jnp.asarray(c) for c in consts])
    parts = lax.all_to_all(terms, "tm", 0, 0, tiled=True)
    return jnp.sum(parts.astype(F32), axis=0).transpose(2, 0, 1, 3)


def solution(mesh):
    in_specs = (P("tm", None, "ap", None),)
    out_specs = P("tm", None, "ap", None)
    return jax.shard_map(shards, mesh=mesh, in_specs=in_specs, out_specs=out_specs, check_vma=False)
```

```python
import functools
import math

import jax
import jax.numpy as jnp
import numpy as np
from jax import lax
from jax.experimental import pallas as pl
from jax.experimental.pallas import tpu as pltpu
from jax.sharding import PartitionSpec as P

F32 = jnp.float32
BF16 = jnp.bfloat16
VMEM_BYTES = 48 * 1024 * 1024


def angles(rows, cols, pad_side):
    return (rows[:, None] * cols[None, :] % pad_side) * (2.0 * math.pi / pad_side)


def split(table):
    table = table.astype(np.float32)
    high = table.astype(BF16)
    return high, (table - high.astype(np.float32)).astype(BF16)


def tables(grid_side, pad_side, samples):
    dishes, index = np.arange(grid_side), np.arange(pad_side)
    padded = angles(dishes, index, pad_side)
    cosine, sine = np.cos(padded), np.sin(padded)
    first = np.block([[cosine, -sine], [sine, cosine]]).astype(BF16)
    second = np.block([[cosine.T, sine.T], [-sine.T, cosine.T]]).astype(BF16)
    by_row = split(np.concatenate([cosine, sine], 0))
    whole = angles(index, index, pad_side)
    by_col = split(np.concatenate([np.cos(whole), np.sin(whole)], 1))
    signed = np.where(index < grid_side, index, index - pad_side)
    pairs = np.maximum(grid_side - np.abs(signed), 0)
    count = pairs[:, None] * pairs[None, :]
    keep = (count > 0) & ((index[:, None] > 0) | (index[None, :] > 0))
    scale = 1.0 / (float(pad_side * pad_side) * np.sqrt(np.maximum(count, 1) * float(samples)))
    factor = np.where(keep, scale, 0.0).astype(np.float32)[:grid_side]
    flip = (dishes[:, None] + dishes[None, :] == grid_side).astype(BF16)
    return first, second, *by_row, *by_col, factor, flip


def dot(a, b):
    return jnp.dot(a, b, preferred_element_type=F32)


def halves(value):
    high = value.astype(BF16)
    return high, (value - high.astype(F32)).astype(BF16)


def dot3(a, b):
    return dot(a[0], b[0]) + (dot(a[0], b[1]) + dot(a[1], b[0]))


def pack(x_ref, out_ref, sems):
    copies = [
        pltpu.make_async_copy(x_ref.at[:, d], out_ref.at[d], sems.at[d])
        for d in range(out_ref.shape[0])
    ]
    for copy in copies:
        copy.start()
    for copy in copies:
        copy.wait()


def rows_of(got_ref, t, c):
    blocks = got_ref[:, t, c].astype(F32)
    count, both, lanes = blocks.shape
    pairs = blocks.reshape(count // 2, 2, both, lanes)
    even, odd = pairs[:, 0], pairs[:, 1]
    upper = lax.broadcasted_iota(jnp.int32, even.shape, 1) < both // 2
    real = jnp.where(upper, even, pltpu.roll(odd, both // 2, 1))
    imag = jnp.where(upper, pltpu.roll(even, both // 2, 1), odd)
    rows = count * both // 2
    return jnp.concatenate([real.reshape(rows, lanes), imag.reshape(rows, lanes)], 1).astype(BF16)


def correlate(
    batch, got_ref, first_ref, second_ref, row_hi, row_lo, col_hi, col_lo, factor_ref, flip_ref, out_ref, power_ref
):
    samples, channels = got_ref.shape[1:3]
    pad = second_ref.shape[1]
    grid_side = pad // 2
    owned = out_ref.shape[3]
    near = grid_side // owned
    power_ref[...] = jnp.zeros_like(power_ref)

    def step(i, carry):
        rows = [rows_of(got_ref, i * batch + t, c) for c in range(channels) for t in range(batch)]
        field = dot(jnp.concatenate(rows, 0), first_ref[...]).astype(BF16)
        for c in range(channels):
            total = power_ref[c]
            for t in range(batch):
                one = field[(c * batch + t) * grid_side : (c * batch + t + 1) * grid_side]
                beam = dot(second_ref[...], jnp.concatenate([one[:, :pad], one[:, pad:]], 0))
                total += beam[:pad] * beam[:pad] + beam[pad:] * beam[pad:]
            power_ref[c] = total
        return carry

    lax.fori_loop(0, samples // batch, step, 0)
    for c in range(channels):
        half = dot3((row_hi[...], row_lo[...]), halves(power_ref[c]))
        both = dot3(halves(half), (col_hi[...], col_lo[...]))
        cos_cos, cos_sin = both[:grid_side, :pad], both[:grid_side, pad:]
        sin_cos, sin_sin = both[grid_side:, :pad], both[grid_side:, pad:]
        plus = (cos_cos - sin_sin, cos_sin + sin_cos)
        minus = (cos_cos + sin_sin, cos_sin - sin_cos)
        for part in range(2):
            lower = (plus[part] * factor_ref[...]).astype(BF16)
            upper = dot(flip_ref[...], (minus[part] * factor_ref[...]).astype(BF16)).astype(BF16)
            out_ref[:near, part, c] = lower.reshape(near, owned, pad)
            out_ref[near:, part, c] = upper.reshape(near, owned, pad)


def shards(voltages):
    samples, channels, local_rows, twice = voltages.shape
    grid_side = twice // 2
    pad_side = 2 * grid_side
    over_ap, over_tm = lax.axis_size("ap"), lax.axis_size("tm")
    own = channels // over_ap
    owned = pad_side // over_tm
    consts = tables(grid_side, pad_side, samples * over_tm)
    vmem = pl.BlockSpec(memory_space=pltpu.VMEM)
    params = pltpu.CompilerParams(vmem_limit_bytes=VMEM_BYTES)
    view = voltages.reshape(samples, over_ap, own, local_rows, 2, grid_side)
    view = view.transpose(0, 1, 2, 4, 3, 5).reshape(samples, over_ap, own, 2 * local_rows, grid_side)
    sent = pl.pallas_call(
        pack,
        out_shape=jax.ShapeDtypeStruct((over_ap, samples) + view.shape[2:], BF16),
        in_specs=[pl.BlockSpec(memory_space=pl.ANY)],
        out_specs=vmem,
        scratch_shapes=[pltpu.SemaphoreType.DMA((over_ap,))],
        compiler_params=params,
        name="pack",
    )(view)
    got = lax.all_to_all(sent, "ap", 0, 0, tiled=True)
    terms = pl.pallas_call(
        functools.partial(correlate, math.gcd(samples, 8)),
        out_shape=jax.ShapeDtypeStruct((over_tm, 2, own, owned, pad_side), BF16),
        in_specs=[vmem] * (1 + len(consts)),
        out_specs=vmem,
        scratch_shapes=[pltpu.VMEM((own, pad_side, pad_side), F32)],
        compiler_params=params,
        name="correlate",
    )(got, *[jnp.asarray(c) for c in consts])
    parts = lax.all_to_all(terms, "tm", 0, 0, tiled=True)
    return jnp.sum(parts.astype(F32), axis=0).transpose(2, 0, 1, 3)


def solution(mesh):
    in_specs = (P("tm", None, "ap", None),)
    out_specs = P("tm", None, "ap", None)
    return jax.shard_map(shards, mesh=mesh, in_specs=in_specs, out_specs=out_specs, check_vma=False)
```

```python
import math

import jax
import jax.numpy as jnp
import numpy as np
from jax import lax
from jax.experimental import pallas as pl
from jax.experimental.pallas import tpu as pltpu
from jax.sharding import PartitionSpec as P

F32 = jnp.float32
BF16 = jnp.bfloat16
VMEM_BYTES = 48 * 1024 * 1024


def angles(rows, cols, pad_side):
    return (rows[:, None] * cols[None, :] % pad_side) * (2.0 * math.pi / pad_side)


def split(table):
    table = table.astype(np.float32)
    high = table.astype(BF16)
    return high, (table - high.astype(np.float32)).astype(BF16)


def tables(grid_side, pad_side, samples):
    dishes, index = np.arange(grid_side), np.arange(pad_side)
    padded = angles(dishes, index, pad_side)
    cosine, sine = np.cos(padded), np.sin(padded)
    first = np.block([[cosine, -sine], [sine, cosine]]).astype(BF16)
    second = np.block([[cosine.T, sine.T], [-sine.T, cosine.T]]).astype(BF16)
    by_row = split(np.concatenate([cosine, sine], 0))
    whole = angles(index, index, pad_side)
    by_col = split(np.concatenate([np.cos(whole), np.sin(whole)], 1))
    signed = np.where(index < grid_side, index, index - pad_side)
    pairs = np.maximum(grid_side - np.abs(signed), 0)
    count = pairs[:, None] * pairs[None, :]
    keep = (count > 0) & ((index[:, None] > 0) | (index[None, :] > 0))
    scale = 1.0 / (float(pad_side * pad_side) * np.sqrt(np.maximum(count, 1) * float(samples)))
    factor = np.where(keep, scale, 0.0).astype(np.float32)[:grid_side]
    flip = (dishes[:, None] + dishes[None, :] == grid_side).astype(BF16)
    return first, second, *by_row, *by_col, factor, flip


def dot(a, b):
    return jnp.dot(a, b, preferred_element_type=F32)


def halves(value):
    high = value.astype(BF16)
    return high, (value - high.astype(F32)).astype(BF16)


def dot3(a, b):
    return dot(a[0], b[0]) + (dot(a[0], b[1]) + dot(a[1], b[0]))


def pack(x_ref, out_ref, sems):
    copies = [
        pltpu.make_async_copy(x_ref.at[:, d], out_ref.at[d], sems.at[d])
        for d in range(out_ref.shape[0])
    ]
    for copy in copies:
        copy.start()
    for copy in copies:
        copy.wait()


def rows_of(got_ref, t, c):
    blocks = got_ref[:, t, c].astype(F32)
    count, both, lanes = blocks.shape
    pairs = blocks.reshape(count // 2, 2, both, lanes)
    even, odd = pairs[:, 0], pairs[:, 1]
    upper = lax.broadcasted_iota(jnp.int32, even.shape, 1) < both // 2
    real = jnp.where(upper, even, pltpu.roll(odd, both // 2, 1))
    imag = jnp.where(upper, pltpu.roll(even, both // 2, 1), odd)
    rows = count * both // 2
    return jnp.concatenate([real.reshape(rows, lanes), imag.reshape(rows, lanes)], 1).astype(BF16)


def power_of(got_ref, first_ref, second_ref, c):
    samples = got_ref.shape[1]
    pad = second_ref.shape[1]
    grid_side = pad // 2
    rows = [rows_of(got_ref, t, c) for t in range(samples)]
    field = dot(jnp.concatenate(rows, 0), first_ref[...]).astype(BF16)
    total = None
    for t in range(samples):
        one = field[t * grid_side : (t + 1) * grid_side]
        beam = dot(second_ref[...], jnp.concatenate([one[:, :pad], one[:, pad:]], 0))
        power = beam[:pad] * beam[:pad] + beam[pad:] * beam[pad:]
        total = power if total is None else total + power
    return total


def correlate(
    got_ref, first_ref, second_ref, row_hi, row_lo, col_hi, col_lo, factor_ref, flip_ref, out_ref, power_ref
):
    channels = got_ref.shape[2]
    pad = second_ref.shape[1]
    grid_side = pad // 2
    owned = out_ref.shape[3]
    near = grid_side // owned
    for c in range(channels):
        power_ref[c] = power_of(got_ref, first_ref, second_ref, c)
    powers = jnp.concatenate([power_ref[c] for c in range(channels)], 1)
    half = dot3((row_hi[...], row_lo[...]), halves(powers))
    half = jnp.concatenate([half[:, c * pad : (c + 1) * pad] for c in range(channels)], 0)
    both = dot3(halves(half), (col_hi[...], col_lo[...]))
    mirrored = []
    for c in range(channels):
        one = both[c * pad : (c + 1) * pad]
        cos_cos, cos_sin = one[:grid_side, :pad], one[:grid_side, pad:]
        sin_cos, sin_sin = one[grid_side:, :pad], one[grid_side:, pad:]
        plus = (cos_cos - sin_sin, cos_sin + sin_cos)
        minus = (cos_cos + sin_sin, cos_sin - sin_cos)
        for part in range(2):
            lower = (plus[part] * factor_ref[...]).astype(BF16)
            out_ref[:near, part, c] = lower.reshape(near, owned, pad)
            mirrored.append((minus[part] * factor_ref[...]).astype(BF16))
    upper = dot(flip_ref[...], jnp.concatenate(mirrored, 1)).astype(BF16)
    for c in range(channels):
        for part in range(2):
            at = (2 * c + part) * pad
            out_ref[near:, part, c] = upper[:, at : at + pad].reshape(near, owned, pad)


def shards(voltages):
    samples, channels, local_rows, twice = voltages.shape
    grid_side = twice // 2
    pad_side = 2 * grid_side
    over_ap, over_tm = lax.axis_size("ap"), lax.axis_size("tm")
    own = channels // over_ap
    owned = pad_side // over_tm
    consts = tables(grid_side, pad_side, samples * over_tm)
    vmem = pl.BlockSpec(memory_space=pltpu.VMEM)
    params = pltpu.CompilerParams(vmem_limit_bytes=VMEM_BYTES)
    view = voltages.reshape(samples, over_ap, own, local_rows, 2, grid_side)
    view = view.transpose(0, 1, 2, 4, 3, 5).reshape(samples, over_ap, own, 2 * local_rows, grid_side)
    sent = pl.pallas_call(
        pack,
        out_shape=jax.ShapeDtypeStruct((over_ap, samples) + view.shape[2:], BF16),
        in_specs=[pl.BlockSpec(memory_space=pltpu.HBM)],
        out_specs=vmem,
        scratch_shapes=[pltpu.SemaphoreType.DMA((over_ap,))],
        compiler_params=params,
        name="pack",
    )(view)
    got = lax.all_to_all(sent, "ap", 0, 0, tiled=True)
    terms = pl.pallas_call(
        correlate,
        out_shape=jax.ShapeDtypeStruct((over_tm, 2, own, owned, pad_side), BF16),
        in_specs=[vmem] * (1 + len(consts)),
        out_specs=vmem,
        scratch_shapes=[pltpu.VMEM((own, pad_side, pad_side), F32)],
        compiler_params=params,
        name="correlate",
    )(got, *[jnp.asarray(c) for c in consts])
    parts = lax.all_to_all(terms, "tm", 0, 0, tiled=True)
    return jnp.sum(parts.astype(F32), axis=0).transpose(2, 0, 1, 3)


def solution(mesh):
    in_specs = (P("tm", None, "ap", None),)
    out_specs = P("tm", None, "ap", None)
    return jax.shard_map(shards, mesh=mesh, in_specs=in_specs, out_specs=out_specs, check_vma=False)
```

```python
import math

import jax
import jax.numpy as jnp
import numpy as np
from jax import lax
from jax.experimental import pallas as pl
from jax.experimental.pallas import tpu as pltpu
from jax.sharding import PartitionSpec as P

F32 = jnp.float32
BF16 = jnp.bfloat16
VMEM_BYTES = 48 * 1024 * 1024


def angles(rows, cols, pad_side):
    return (rows[:, None] * cols[None, :] % pad_side) * (2.0 * math.pi / pad_side)


def split(table):
    table = table.astype(np.float32)
    high = table.astype(BF16)
    return high, (table - high.astype(np.float32)).astype(BF16)


def tables(grid_side, pad_side, samples):
    dishes, index = np.arange(grid_side), np.arange(pad_side)
    padded = angles(dishes, index, pad_side)
    cosine, sine = np.cos(padded), np.sin(padded)
    first = np.block([[cosine, -sine], [sine, cosine]]).astype(BF16)
    second = np.block([[cosine.T, sine.T], [-sine.T, cosine.T]]).astype(BF16)
    by_row = split(np.concatenate([cosine, sine], 0))
    whole = angles(index, index, pad_side)
    by_col = split(np.concatenate([np.cos(whole), np.sin(whole)], 1))
    signed = np.where(index < grid_side, index, index - pad_side)
    pairs = np.maximum(grid_side - np.abs(signed), 0)
    count = pairs[:, None] * pairs[None, :]
    keep = (count > 0) & ((index[:, None] > 0) | (index[None, :] > 0))
    scale = 1.0 / (float(pad_side * pad_side) * np.sqrt(np.maximum(count, 1) * float(samples)))
    factor = np.where(keep, scale, 0.0).astype(np.float32)[:grid_side]
    flip = (dishes[:, None] + dishes[None, :] == grid_side).astype(BF16)
    return first, second, *by_row, *by_col, factor, flip


def dot(a, b):
    return jnp.dot(a, b, preferred_element_type=F32)


def halves(value):
    high = value.astype(BF16)
    return high, (value - high.astype(F32)).astype(BF16)


def dot3(a, b):
    return dot(a[0], b[0]) + (dot(a[0], b[1]) + dot(a[1], b[0]))


def pack(x_ref, out_ref, sems):
    copies = [
        pltpu.make_async_copy(x_ref.at[:, d], out_ref.at[d], sems.at[d])
        for d in range(out_ref.shape[0])
    ]
    for copy in copies:
        copy.start()
    for copy in copies:
        copy.wait()


def rows_of(got_ref, t, c):
    blocks = got_ref[:, t, c].astype(F32)
    count, both, lanes = blocks.shape
    pairs = blocks.reshape(count // 2, 2, both, lanes)
    even, odd = pairs[:, 0], pairs[:, 1]
    upper = lax.broadcasted_iota(jnp.int32, even.shape, 1) < both // 2
    real = jnp.where(upper, even, pltpu.roll(odd, both // 2, 1))
    imag = jnp.where(upper, pltpu.roll(even, both // 2, 1), odd)
    rows = count * both // 2
    return jnp.concatenate([real.reshape(rows, lanes), imag.reshape(rows, lanes)], 1).astype(BF16)


def power_of(got_ref, first_ref, second_ref, c):
    samples = got_ref.shape[1]
    pad = second_ref.shape[1]
    grid_side = pad // 2
    rows = [rows_of(got_ref, t, c) for t in range(samples)]
    field = dot(jnp.concatenate(rows, 0), first_ref[...]).astype(BF16)
    total = None
    for t in range(samples):
        one = field[t * grid_side : (t + 1) * grid_side]
        beam = dot(second_ref[...], jnp.concatenate([one[:, :pad], one[:, pad:]], 0))
        power = beam[:pad] * beam[:pad] + beam[pad:] * beam[pad:]
        total = power if total is None else total + power
    return total


def correlate(
    got_ref, first_ref, second_ref, row_hi, row_lo, col_hi, col_lo, factor_ref, flip_ref, out_ref, power_ref
):
    channels = got_ref.shape[2]
    pad = second_ref.shape[1]
    grid_side = pad // 2
    owned = out_ref.shape[3]
    near = grid_side // owned
    for c in range(channels):
        power_ref[c] = power_of(got_ref, first_ref, second_ref, c)
    powers = jnp.concatenate([power_ref[c] for c in range(channels)], 1)
    half = dot3((row_hi[...], row_lo[...]), halves(powers))
    half = jnp.concatenate([half[:, c * pad : (c + 1) * pad] for c in range(channels)], 0)
    both = dot3(halves(half), (col_hi[...], col_lo[...]))
    mirrored = []
    for c in range(channels):
        one = both[c * pad : (c + 1) * pad]
        cos_cos, cos_sin = one[:grid_side, :pad], one[:grid_side, pad:]
        sin_cos, sin_sin = one[grid_side:, :pad], one[grid_side:, pad:]
        plus = (cos_cos - sin_sin, cos_sin + sin_cos)
        minus = (cos_cos + sin_sin, cos_sin - sin_cos)
        for part in range(2):
            lower = (plus[part] * factor_ref[...]).astype(BF16)
            out_ref[:near, part, c] = lower.reshape(near, owned, pad)
            mirrored.append((minus[part] * factor_ref[...]).astype(BF16))
    upper = dot(flip_ref[...], jnp.concatenate(mirrored, 1)).astype(BF16)
    for c in range(channels):
        for part in range(2):
            at = (2 * c + part) * pad
            out_ref[near:, part, c] = upper[:, at : at + pad].reshape(near, owned, pad)


def shards(voltages):
    samples, channels, local_rows, twice = voltages.shape
    grid_side = twice // 2
    pad_side = 2 * grid_side
    over_ap, over_tm = lax.axis_size("ap"), lax.axis_size("tm")
    own = channels // over_ap
    owned = pad_side // over_tm
    consts = tables(grid_side, pad_side, samples * over_tm)
    vmem = pl.BlockSpec(memory_space=pltpu.VMEM)
    params = pltpu.CompilerParams(vmem_limit_bytes=VMEM_BYTES)
    view = voltages.reshape(samples, over_ap, own, local_rows, 2, grid_side)
    view = view.transpose(0, 1, 2, 4, 3, 5).reshape(samples, over_ap, own, 2 * local_rows, grid_side)
    sent = pl.pallas_call(
        pack,
        out_shape=pltpu.VMEM((over_ap, samples) + view.shape[2:], BF16),
        in_specs=[pl.BlockSpec(memory_space=pltpu.HBM)],
        out_specs=vmem,
        scratch_shapes=[pltpu.SemaphoreType.DMA((over_ap,))],
        compiler_params=params,
        name="pack",
    )(pltpu.with_memory_space_constraint(view, pltpu.HBM))
    got = lax.all_to_all(sent, "ap", 0, 0, tiled=True)
    terms = pl.pallas_call(
        correlate,
        out_shape=jax.ShapeDtypeStruct((over_tm, 2, own, owned, pad_side), BF16),
        in_specs=[vmem] * (1 + len(consts)),
        out_specs=vmem,
        scratch_shapes=[pltpu.VMEM((own, pad_side, pad_side), F32)],
        compiler_params=params,
        name="correlate",
    )(got, *[jnp.asarray(c) for c in consts])
    parts = lax.all_to_all(terms, "tm", 0, 0, tiled=True)
    return jnp.sum(parts.astype(F32), axis=0).transpose(2, 0, 1, 3)


def solution(mesh):
    in_specs = (P("tm", None, "ap", None),)
    out_specs = P("tm", None, "ap", None)
    return jax.shard_map(shards, mesh=mesh, in_specs=in_specs, out_specs=out_specs, check_vma=False)
```

```python
import math

import jax
import jax.numpy as jnp
import numpy as np
from jax import lax
from jax.experimental import pallas as pl
from jax.experimental.pallas import tpu as pltpu
from jax.sharding import PartitionSpec as P

F32 = jnp.float32
BF16 = jnp.bfloat16
VMEM_BYTES = 48 * 1024 * 1024


def angles(rows, cols, pad_side):
    return (rows[:, None] * cols[None, :] % pad_side) * (2.0 * math.pi / pad_side)


def split(table):
    table = table.astype(np.float32)
    high = table.astype(BF16)
    return high, (table - high.astype(np.float32)).astype(BF16)


def tables(grid_side, pad_side, samples):
    dishes, index = np.arange(grid_side), np.arange(pad_side)
    padded = angles(dishes, index, pad_side)
    cosine, sine = np.cos(padded), np.sin(padded)
    first = np.block([[cosine, -sine], [sine, cosine]]).astype(BF16)
    second = np.block([[cosine.T, sine.T], [-sine.T, cosine.T]]).astype(BF16)
    by_row = split(np.concatenate([cosine, sine], 0))
    whole = angles(index, index, pad_side)
    by_col = split(np.concatenate([np.cos(whole), np.sin(whole)], 1))
    signed = np.where(index < grid_side, index, index - pad_side)
    pairs = np.maximum(grid_side - np.abs(signed), 0)
    count = pairs[:, None] * pairs[None, :]
    keep = (count > 0) & ((index[:, None] > 0) | (index[None, :] > 0))
    scale = 1.0 / (float(pad_side * pad_side) * np.sqrt(np.maximum(count, 1) * float(samples)))
    factor = np.where(keep, scale, 0.0).astype(np.float32)[:grid_side]
    flip = (dishes[:, None] + dishes[None, :] == grid_side).astype(BF16)
    return first, second, *by_row, *by_col, factor, flip


def dot(a, b):
    return jnp.dot(a, b, preferred_element_type=F32)


def halves(value):
    high = value.astype(BF16)
    return high, (value - high.astype(F32)).astype(BF16)


def dot3(a, b):
    return dot(a[0], b[0]) + (dot(a[0], b[1]) + dot(a[1], b[0]))


def pack(x_ref, out_ref, sems):
    copies = [
        pltpu.make_async_copy(x_ref.at[:, d], out_ref.at[d], sems.at[d])
        for d in range(out_ref.shape[0])
    ]
    for copy in copies:
        copy.start()
    for copy in copies:
        copy.wait()


def rows_of(got_ref, sample):
    blocks = got_ref[(slice(None),) + sample].astype(F32)
    count, both, lanes = blocks.shape
    pairs = blocks.reshape(count // 2, 2, both, lanes)
    even, odd = pairs[:, 0], pairs[:, 1]
    upper = lax.broadcasted_iota(jnp.int32, even.shape, 1) < both // 2
    real = jnp.where(upper, even, pltpu.roll(odd, both // 2, 1))
    imag = jnp.where(upper, pltpu.roll(even, both // 2, 1), odd)
    rows = count * both // 2
    return jnp.concatenate([real.reshape(rows, lanes), imag.reshape(rows, lanes)], 1).astype(BF16)


def power_of(got_ref, first_ref, second_ref, part):
    samples = got_ref.shape[2]
    pad = second_ref.shape[1]
    grid_side = pad // 2
    rows = [rows_of(got_ref, (part, t)) for t in range(samples)]
    field = dot(jnp.concatenate(rows, 0), first_ref[...]).astype(BF16)
    total = None
    for t in range(samples):
        one = field[t * grid_side : (t + 1) * grid_side]
        beam = dot(second_ref[...], jnp.concatenate([one[:, :pad], one[:, pad:]], 0))
        power = beam[:pad] * beam[:pad] + beam[pad:] * beam[pad:]
        total = power if total is None else total + power
    return total


def correlate(
    got_ref, first_ref, second_ref, row_hi, row_lo, col_hi, col_lo, factor_ref, flip_ref, out_ref, power_ref
):
    pad = second_ref.shape[1]
    grid_side = pad // 2
    owned = out_ref.shape[2]
    near = grid_side // owned
    for part in range(got_ref.shape[1]):
        power = power_of(got_ref, first_ref, second_ref, part)
        power_ref[...] = power if part == 0 else power_ref[...] + power
    half = dot3((row_hi[...], row_lo[...]), halves(power_ref[...]))
    both = dot3(halves(half), (col_hi[...], col_lo[...]))
    cos_cos, cos_sin = both[:grid_side, :pad], both[:grid_side, pad:]
    sin_cos, sin_sin = both[grid_side:, :pad], both[grid_side:, pad:]
    plus = (cos_cos - sin_sin, cos_sin + sin_cos)
    minus = (cos_cos + sin_sin, cos_sin - sin_cos)
    mirrored = [(m * factor_ref[...]).astype(BF16) for m in minus]
    upper = dot(flip_ref[...], jnp.concatenate(mirrored, 1)).astype(BF16)
    for part in range(2):
        lower = (plus[part] * factor_ref[...]).astype(BF16)
        out_ref[:near, part] = lower.reshape(near, owned, pad)
        out_ref[near:, part] = upper[:, part * pad : (part + 1) * pad].reshape(near, owned, pad)


def shards(voltages):
    samples, channels, local_rows, twice = voltages.shape
    grid_side = twice // 2
    pad_side = 2 * grid_side
    over_ap, over_tm = lax.axis_size("ap"), lax.axis_size("tm")
    own = channels // over_ap
    owned = pad_side // over_tm
    consts = tables(grid_side, pad_side, samples * over_tm)
    vmem = pl.BlockSpec(memory_space=pltpu.VMEM)
    params = pltpu.CompilerParams(vmem_limit_bytes=VMEM_BYTES)
    view = voltages.reshape(samples, channels, local_rows, 2, grid_side)
    view = view.transpose(0, 1, 3, 2, 4).reshape(samples, channels, 2 * local_rows, grid_side)
    sent = pl.pallas_call(
        pack,
        out_shape=pltpu.VMEM((channels, samples) + view.shape[2:], BF16),
        in_specs=[pl.BlockSpec(memory_space=pltpu.HBM)],
        out_specs=vmem,
        scratch_shapes=[pltpu.SemaphoreType.DMA((channels,))],
        compiler_params=params,
        name="pack",
    )(pltpu.with_memory_space_constraint(view, pltpu.HBM))
    groups = [
        [t * over_ap + a for a in range(over_ap) for t in range(run, run + own)]
        for run in range(0, over_tm, own)
    ]
    got = lax.all_to_all(sent, ("tm", "ap"), 0, 0, axis_index_groups=groups, tiled=True)
    got = got.reshape((over_ap, own) + got.shape[1:])
    terms = pl.pallas_call(
        correlate,
        out_shape=jax.ShapeDtypeStruct((over_tm, 2, owned, pad_side), BF16),
        in_specs=[vmem] * (1 + len(consts)),
        out_specs=vmem,
        scratch_shapes=[pltpu.VMEM((pad_side, pad_side), F32)],
        compiler_params=params,
        name="correlate",
    )(got, *[jnp.asarray(c) for c in consts])
    parts = lax.all_to_all(terms, "tm", 0, 0, tiled=True)
    parts = parts.reshape((over_tm // own, own) + parts.shape[1:])
    return jnp.sum(parts.astype(F32), axis=0).transpose(2, 1, 0, 3)


def solution(mesh):
    in_specs = (P("tm", None, "ap", None),)
    out_specs = P("tm", None, "ap", None)
    return jax.shard_map(shards, mesh=mesh, in_specs=in_specs, out_specs=out_specs, check_vma=False)
```

```python
import functools
import math

import jax
import jax.numpy as jnp
import numpy as np
from jax import lax
from jax.experimental import pallas as pl
from jax.experimental.pallas import tpu as pltpu
from jax.sharding import PartitionSpec as P

F32 = jnp.float32
BF16 = jnp.bfloat16
VMEM_BYTES = 48 * 1024 * 1024
ORDER = (
    46, 20, 15, 26, 49, 35, 61, 0, 12, 56, 53, 18, 41, 7, 27, 38,
    30, 19, 33, 63, 10, 48, 45, 4, 37, 11, 25, 55, 2, 22, 40, 60,
    47, 3, 29, 32, 17, 52, 14, 58, 59, 6, 21, 39, 9, 24, 44, 50,
    13, 42, 31, 1, 62, 51, 36, 16, 28, 57, 8, 23, 54, 43, 34, 5,
)


def angles(rows, cols, pad_side):
    return (rows[:, None] * cols[None, :] % pad_side) * (2.0 * math.pi / pad_side)


def split(table):
    table = table.astype(np.float32)
    high = table.astype(BF16)
    return high, (table - high.astype(np.float32)).astype(BF16)


def tables(grid_side, pad_side, samples):
    dishes, index = np.arange(grid_side), np.arange(pad_side)
    padded = angles(dishes, index, pad_side)
    cosine, sine = np.cos(padded), np.sin(padded)
    first = np.block([[cosine, -sine], [sine, cosine]]).astype(BF16)
    second = np.block([[cosine.T, sine.T], [-sine.T, cosine.T]]).astype(BF16)
    high, low = split(np.concatenate([cosine, sine], 0))
    by_row = np.concatenate([high, high, low], 1)
    whole = angles(index, index, pad_side)
    high, low = split(np.concatenate([np.cos(whole), np.sin(whole)], 1))
    by_col = np.concatenate([high, low, high], 0)
    signed = np.where(index < grid_side, index, index - pad_side)
    pairs = np.maximum(grid_side - np.abs(signed), 0)
    count = pairs[:, None] * pairs[None, :]
    keep = (count > 0) & ((index[:, None] > 0) | (index[None, :] > 0))
    scale = 1.0 / (float(pad_side * pad_side) * np.sqrt(np.maximum(count, 1) * float(samples)))
    factor = np.where(keep, scale, 0.0).astype(np.float32)[:grid_side]
    flip = (dishes[:, None] + dishes[None, :] == grid_side).astype(BF16)
    return first, second, by_row, by_col, factor, flip


def dot(a, b):
    return jnp.dot(a, b, preferred_element_type=F32)


def halves(value):
    high = value.astype(BF16)
    return high, (value - high.astype(F32)).astype(BF16)


def pack(order, x_ref, out_ref, sems):
    copies = [
        pltpu.make_async_copy(x_ref.at[:, channel], out_ref.at[slot], sems.at[slot])
        for slot, channel in enumerate(order)
    ]
    for copy in copies:
        copy.start()
    for copy in copies:
        copy.wait()


def rows_of(got_ref, slots, t):
    even = jnp.stack([got_ref[slot, t].astype(F32) for slot in slots[0::2]])
    odd = jnp.stack([got_ref[slot, t].astype(F32) for slot in slots[1::2]])
    count, both, lanes = even.shape
    upper = lax.broadcasted_iota(jnp.int32, even.shape, 1) < both // 2
    real = jnp.where(upper, even, pltpu.roll(odd, both // 2, 1))
    imag = jnp.where(upper, pltpu.roll(even, both // 2, 1), odd)
    rows = count * both
    return jnp.concatenate([real.reshape(rows, lanes), imag.reshape(rows, lanes)], 1).astype(BF16)


def power_of(got_ref, first_ref, second_ref, slots):
    samples = got_ref.shape[1]
    pad = second_ref.shape[1]
    grid_side = pad // 2
    rows = [rows_of(got_ref, slots, t) for t in range(samples)]
    field = dot(jnp.concatenate(rows, 0), first_ref[...]).astype(BF16)
    total = None
    for t in range(samples):
        one = field[t * grid_side : (t + 1) * grid_side]
        beam = dot(second_ref[...], jnp.concatenate([one[:, :pad], one[:, pad:]], 0))
        power = beam[:pad] * beam[:pad] + beam[pad:] * beam[pad:]
        total = power if total is None else total + power
    return total


def correlate(slots, got_ref, first_ref, second_ref, by_row, by_col, factor_ref, flip_ref, out_ref, power_ref):
    pad = second_ref.shape[1]
    grid_side = pad // 2
    owned = out_ref.shape[2]
    near = grid_side // owned
    for part, places in enumerate(slots):
        power = power_of(got_ref, first_ref, second_ref, places)
        power_ref[...] = power if part == 0 else power_ref[...] + power
    high, low = halves(power_ref[...])
    half = dot(by_row[...], jnp.concatenate([high, low, high], 0))
    high, low = halves(half)
    both = dot(jnp.concatenate([high, high, low], 1), by_col[...])
    cos_cos, cos_sin = both[:grid_side, :pad], both[:grid_side, pad:]
    sin_cos, sin_sin = both[grid_side:, :pad], both[grid_side:, pad:]
    plus = (cos_cos - sin_sin, cos_sin + sin_cos)
    minus = (cos_cos + sin_sin, cos_sin - sin_cos)
    mirrored = [(m * factor_ref[...]).astype(BF16) for m in minus]
    upper = dot(flip_ref[...], jnp.concatenate(mirrored, 1)).astype(BF16)
    for part in range(2):
        lower = (plus[part] * factor_ref[...]).astype(BF16)
        out_ref[:near, part] = lower.reshape(near, owned, pad)
        out_ref[near:, part] = upper[:, part * pad : (part + 1) * pad].reshape(near, owned, pad)


def shards(voltages):
    samples, channels, local_rows, twice = voltages.shape
    grid_side = twice // 2
    pad_side = 2 * grid_side
    over_ap, over_tm = lax.axis_size("ap"), lax.axis_size("tm")
    own = channels // over_ap
    owned = pad_side // over_tm
    consts = tables(grid_side, pad_side, samples * over_tm)
    vmem = pl.BlockSpec(memory_space=pltpu.VMEM)
    params = pltpu.CompilerParams(vmem_limit_bytes=VMEM_BYTES)
    view = voltages.reshape(samples, channels, local_rows, 2, grid_side)
    view = view.transpose(0, 1, 3, 2, 4).reshape(samples, channels, 2 * local_rows, grid_side)
    order = ORDER if len(ORDER) == channels else tuple(range(channels))
    sent = pl.pallas_call(
        functools.partial(pack, order),
        out_shape=pltpu.VMEM((channels, samples) + view.shape[2:], BF16),
        in_specs=[pl.BlockSpec(memory_space=pltpu.HBM)],
        out_specs=vmem,
        scratch_shapes=[pltpu.SemaphoreType.DMA((channels,))],
        compiler_params=params,
        name="pack",
    )(pltpu.with_memory_space_constraint(view, pltpu.HBM))
    groups = [
        [(run + channel % own) * over_ap + channel // own for channel in order]
        for run in range(0, over_tm, own)
    ]
    slots = [[order.index(a * own + p) for a in range(over_ap)] for p in range(own)]
    got = lax.all_to_all(sent, ("tm", "ap"), 0, 0, axis_index_groups=groups, tiled=True)
    terms = pl.pallas_call(
        functools.partial(correlate, slots),
        out_shape=jax.ShapeDtypeStruct((over_tm, 2, owned, pad_side), BF16),
        in_specs=[vmem] * (1 + len(consts)),
        out_specs=vmem,
        scratch_shapes=[pltpu.VMEM((pad_side, pad_side), F32)],
        compiler_params=params,
        name="correlate",
    )(got, *[jnp.asarray(c) for c in consts])
    parts = lax.all_to_all(terms, "tm", 0, 0, tiled=True)
    parts = parts.reshape((over_tm // own, own) + parts.shape[1:])
    return jnp.sum(parts.astype(F32), axis=0).transpose(2, 1, 0, 3)


def solution(mesh):
    in_specs = (P("tm", None, "ap", None),)
    out_specs = P("tm", None, "ap", None)
    return jax.shard_map(shards, mesh=mesh, in_specs=in_specs, out_specs=out_specs, check_vma=False)
```

```python
import functools
import math

import jax
import jax.numpy as jnp
import numpy as np
from jax import lax
from jax.experimental import pallas as pl
from jax.experimental.pallas import tpu as pltpu
from jax.sharding import PartitionSpec as P

F32 = jnp.float32
BF16 = jnp.bfloat16
VMEM_BYTES = 48 * 1024 * 1024
ORDER = (
    46, 20, 15, 26, 49, 35, 61, 0, 12, 56, 53, 18, 41, 7, 27, 34,
    43, 54, 23, 8, 57, 28, 16, 36, 51, 62, 1, 31, 42, 13, 50, 44,
    24, 9, 39, 21, 6, 59, 58, 14, 55, 22, 40, 60, 47, 3, 29, 32,
    17, 52, 2, 25, 11, 37, 4, 45, 48, 10, 63, 33, 19, 30, 38, 5,
)
LAST_ORDER = (4, 1, 6, 2, 3, 7, 5, 0)


def angles(rows, cols, pad_side):
    return (rows[:, None] * cols[None, :] % pad_side) * (2.0 * math.pi / pad_side)


def split(table):
    table = table.astype(np.float32)
    high = table.astype(BF16)
    return high, (table - high.astype(np.float32)).astype(BF16)


def tables(grid_side, pad_side, samples):
    dishes, index = np.arange(grid_side), np.arange(pad_side)
    padded = angles(dishes, index, pad_side)
    cosine, sine = np.cos(padded), np.sin(padded)
    first = np.block([[cosine, -sine], [sine, cosine]]).astype(BF16)
    second = np.block([[cosine.T, sine.T], [-sine.T, cosine.T]]).astype(BF16)
    high, low = split(np.concatenate([cosine, sine], 0))
    by_row = np.concatenate([high, high, low], 1)
    whole = angles(index, index, pad_side)
    high, low = split(np.concatenate([np.cos(whole), np.sin(whole)], 1))
    by_col = np.concatenate([high, low, high], 0)
    signed = np.where(index < grid_side, index, index - pad_side)
    pairs = np.maximum(grid_side - np.abs(signed), 0)
    count = pairs[:, None] * pairs[None, :]
    keep = (count > 0) & ((index[:, None] > 0) | (index[None, :] > 0))
    scale = 1.0 / (float(pad_side * pad_side) * np.sqrt(np.maximum(count, 1) * float(samples)))
    factor = np.where(keep, scale, 0.0).astype(np.float32)[:grid_side]
    flip = (dishes[:, None] + dishes[None, :] == grid_side).astype(BF16)
    return first, second, by_row, by_col, factor, flip


def dot(a, b):
    return jnp.dot(a, b, preferred_element_type=F32)


def halves(value):
    high = value.astype(BF16)
    return high, (value - high.astype(F32)).astype(BF16)


def pack(order, x_ref, out_ref, sems):
    copies = [
        pltpu.make_async_copy(x_ref.at[:, channel], out_ref.at[slot], sems.at[slot])
        for slot, channel in enumerate(order)
    ]
    for copy in copies:
        copy.start()
    for copy in copies:
        copy.wait()


def rows_of(got_ref, slots, t):
    even = jnp.stack([got_ref[slot, t].astype(F32) for slot in slots[0::2]])
    odd = jnp.stack([got_ref[slot, t].astype(F32) for slot in slots[1::2]])
    count, both, lanes = even.shape
    upper = lax.broadcasted_iota(jnp.int32, even.shape, 1) < both // 2
    real = jnp.where(upper, even, pltpu.roll(odd, both // 2, 1))
    imag = jnp.where(upper, pltpu.roll(even, both // 2, 1), odd)
    rows = count * both
    return jnp.concatenate([real.reshape(rows, lanes), imag.reshape(rows, lanes)], 1).astype(BF16)


def power_of(got_ref, first_ref, second_ref, slots):
    samples = got_ref.shape[1]
    pad = second_ref.shape[1]
    grid_side = pad // 2
    rows = [rows_of(got_ref, slots, t) for t in range(samples)]
    field = dot(jnp.concatenate(rows, 0), first_ref[...]).astype(BF16)
    total = None
    for t in range(samples):
        one = field[t * grid_side : (t + 1) * grid_side]
        beam = dot(second_ref[...], jnp.concatenate([one[:, :pad], one[:, pad:]], 0))
        power = beam[:pad] * beam[:pad] + beam[pad:] * beam[pad:]
        total = power if total is None else total + power
    return total


def correlate(slots, places, got_ref, first_ref, second_ref, by_row, by_col, factor_ref, flip_ref, out_ref, power_ref):
    pad = second_ref.shape[1]
    grid_side = pad // 2
    owned = out_ref.shape[2]
    near = grid_side // owned
    for part, senders in enumerate(slots):
        power = power_of(got_ref, first_ref, second_ref, senders)
        power_ref[...] = power if part == 0 else power_ref[...] + power
    high, low = halves(power_ref[...])
    half = dot(by_row[...], jnp.concatenate([high, low, high], 0))
    high, low = halves(half)
    both = dot(jnp.concatenate([high, high, low], 1), by_col[...])
    cos_cos, cos_sin = both[:grid_side, :pad], both[:grid_side, pad:]
    sin_cos, sin_sin = both[grid_side:, :pad], both[grid_side:, pad:]
    plus = (cos_cos - sin_sin, cos_sin + sin_cos)
    minus = (cos_cos + sin_sin, cos_sin - sin_cos)
    mirrored = [(m * factor_ref[...]).astype(BF16) for m in minus]
    upper = dot(flip_ref[...], jnp.concatenate(mirrored, 1)).astype(BF16)
    for part in range(2):
        lower = (plus[part] * factor_ref[...]).astype(BF16)
        for i in range(near):
            out_ref[places[i], part] = lower[i * owned : (i + 1) * owned]
            out_ref[places[near + i], part] = upper[i * owned : (i + 1) * owned, part * pad : (part + 1) * pad]


def shards(voltages):
    samples, channels, local_rows, twice = voltages.shape
    grid_side = twice // 2
    pad_side = 2 * grid_side
    over_ap, over_tm = lax.axis_size("ap"), lax.axis_size("tm")
    own = channels // over_ap
    owned = pad_side // over_tm
    consts = tables(grid_side, pad_side, samples * over_tm)
    vmem = pl.BlockSpec(memory_space=pltpu.VMEM)
    params = pltpu.CompilerParams(vmem_limit_bytes=VMEM_BYTES)
    view = voltages.reshape(samples, channels, local_rows, 2, grid_side)
    view = view.transpose(0, 1, 3, 2, 4).reshape(samples, channels, 2 * local_rows, grid_side)
    order = ORDER if len(ORDER) == channels else tuple(range(channels))
    sent = pl.pallas_call(
        functools.partial(pack, order),
        out_shape=pltpu.VMEM((channels, samples) + view.shape[2:], BF16),
        in_specs=[pl.BlockSpec(memory_space=pltpu.HBM)],
        out_specs=vmem,
        scratch_shapes=[pltpu.SemaphoreType.DMA((channels,))],
        compiler_params=params,
        name="pack",
    )(pltpu.with_memory_space_constraint(view, pltpu.HBM))
    groups = [
        [(run + channel % own) * over_ap + channel // own for channel in order]
        for run in range(0, over_tm, own)
    ]
    slots = [[order.index(a * own + p) for a in range(over_ap)] for p in range(own)]
    got = lax.all_to_all(sent, ("tm", "ap"), 0, 0, axis_index_groups=groups, tiled=True)
    last = LAST_ORDER if len(LAST_ORDER) == over_tm else tuple(range(over_tm))
    terms = pl.pallas_call(
        functools.partial(correlate, slots, [last.index(t) for t in range(over_tm)]),
        out_shape=jax.ShapeDtypeStruct((over_tm, 2, owned, pad_side), BF16),
        in_specs=[vmem] * (1 + len(consts)),
        out_specs=vmem,
        scratch_shapes=[pltpu.VMEM((pad_side, pad_side), F32)],
        compiler_params=params,
        name="correlate",
    )(got, *[jnp.asarray(c) for c in consts])
    parts = lax.all_to_all(terms, "tm", 0, 0, axis_index_groups=[list(last)], tiled=True)
    sums = [
        sum(parts[i].astype(F32) for i, t in enumerate(last) if t % own == p) for p in range(own)
    ]
    return jnp.stack(sums, 0).transpose(2, 1, 0, 3)


def solution(mesh):
    in_specs = (P("tm", None, "ap", None),)
    out_specs = P("tm", None, "ap", None)
    return jax.shard_map(shards, mesh=mesh, in_specs=in_specs, out_specs=out_specs, check_vma=False)
```

```python
import functools
import math

import jax
import jax.numpy as jnp
import numpy as np
from jax import lax
from jax.experimental import pallas as pl
from jax.experimental.pallas import tpu as pltpu
from jax.sharding import PartitionSpec as P

F32 = jnp.float32
BF16 = jnp.bfloat16
VMEM_BYTES = 48 * 1024 * 1024
ORDER = (
    46, 20, 15, 26, 48, 29, 61, 0, 12, 56, 8, 18, 31, 7, 4, 17,
    43, 54, 23, 53, 57, 28, 16, 36, 51, 62, 1, 41, 63, 13, 50, 10,
    24, 9, 39, 27, 21, 6, 38, 58, 14, 52, 34, 32, 35, 3, 60, 47,
    22, 40, 2, 55, 25, 19, 37, 45, 49, 44, 42, 5, 11, 30, 59, 33,
)
LAST_ORDER = (4, 1, 6, 2, 3, 7, 5, 0)


def angles(rows, cols, pad_side):
    return (rows[:, None] * cols[None, :] % pad_side) * (2.0 * math.pi / pad_side)


def split(table):
    table = table.astype(np.float32)
    high = table.astype(BF16)
    return high, (table - high.astype(np.float32)).astype(BF16)


def tables(grid_side, pad_side, samples):
    dishes, index = np.arange(grid_side), np.arange(pad_side)
    padded = angles(dishes, index, pad_side)
    cosine, sine = np.cos(padded), np.sin(padded)
    first = np.block([[cosine, -sine], [sine, cosine]]).astype(BF16)
    second = np.block([[cosine.T, sine.T], [-sine.T, cosine.T]]).astype(BF16)
    high, low = split(np.concatenate([cosine, sine], 0))
    by_row = np.concatenate([high, high, low], 1)
    whole = angles(index, index, pad_side)
    high, low = split(np.concatenate([np.cos(whole), np.sin(whole)], 1))
    by_col = np.concatenate([high, low, high], 0)
    signed = np.where(index < grid_side, index, index - pad_side)
    pairs = np.maximum(grid_side - np.abs(signed), 0)
    count = pairs[:, None] * pairs[None, :]
    keep = (count > 0) & ((index[:, None] > 0) | (index[None, :] > 0))
    scale = 1.0 / (float(pad_side * pad_side) * np.sqrt(np.maximum(count, 1) * float(samples)))
    factor = np.where(keep, scale, 0.0).astype(np.float32)[:grid_side]
    flip = (dishes[:, None] + dishes[None, :] == grid_side).astype(BF16)
    return first, second, by_row, by_col, factor, flip


def dot(a, b):
    return jnp.dot(a, b, preferred_element_type=F32)


def halves(value):
    high = value.astype(BF16)
    return high, (value - high.astype(F32)).astype(BF16)


def pack(order, x_ref, out_ref, held_ref, sems):
    copies = [
        pltpu.make_async_copy(x_ref.at[t], held_ref.at[t], sems.at[t])
        for t in range(x_ref.shape[0])
    ]
    for copy in copies:
        copy.start()
    for t, copy in enumerate(copies):
        copy.wait()
        for slot, channel in enumerate(order):
            out_ref[slot, t] = held_ref[t, channel]


def rows_of(got_ref, slots, t):
    even = jnp.stack([got_ref[slot, t].astype(F32) for slot in slots[0::2]])
    odd = jnp.stack([got_ref[slot, t].astype(F32) for slot in slots[1::2]])
    count, both, lanes = even.shape
    upper = lax.broadcasted_iota(jnp.int32, even.shape, 1) < both // 2
    real = jnp.where(upper, even, pltpu.roll(odd, both // 2, 1))
    imag = jnp.where(upper, pltpu.roll(even, both // 2, 1), odd)
    rows = count * both
    return jnp.concatenate([real.reshape(rows, lanes), imag.reshape(rows, lanes)], 1).astype(BF16)


def power_of(got_ref, first_ref, second_ref, slots):
    samples = got_ref.shape[1]
    pad = second_ref.shape[1]
    grid_side = pad // 2
    rows = [rows_of(got_ref, slots, t) for t in range(samples)]
    field = dot(jnp.concatenate(rows, 0), first_ref[...]).astype(BF16)
    total = None
    for t in range(samples):
        one = field[t * grid_side : (t + 1) * grid_side]
        beam = dot(second_ref[...], jnp.concatenate([one[:, :pad], one[:, pad:]], 0))
        power = beam[:pad] * beam[:pad] + beam[pad:] * beam[pad:]
        total = power if total is None else total + power
    return total


def correlate(slots, places, got_ref, first_ref, second_ref, by_row, by_col, factor_ref, flip_ref, out_ref, power_ref):
    pad = second_ref.shape[1]
    grid_side = pad // 2
    owned = out_ref.shape[2]
    near = grid_side // owned
    for part, senders in enumerate(slots):
        power = power_of(got_ref, first_ref, second_ref, senders)
        power_ref[...] = power if part == 0 else power_ref[...] + power
    high, low = halves(power_ref[...])
    half = dot(by_row[...], jnp.concatenate([high, low, high], 0))
    high, low = halves(half)
    both = dot(jnp.concatenate([high, high, low], 1), by_col[...])
    cos_cos, cos_sin = both[:grid_side, :pad], both[:grid_side, pad:]
    sin_cos, sin_sin = both[grid_side:, :pad], both[grid_side:, pad:]
    plus = (cos_cos - sin_sin, cos_sin + sin_cos)
    minus = (cos_cos + sin_sin, cos_sin - sin_cos)
    mirrored = [(m * factor_ref[...]).astype(BF16) for m in minus]
    upper = dot(flip_ref[...], jnp.concatenate(mirrored, 1)).astype(BF16)
    for part in range(2):
        lower = (plus[part] * factor_ref[...]).astype(BF16)
        for i in range(near):
            out_ref[places[i], part] = lower[i * owned : (i + 1) * owned]
            out_ref[places[near + i], part] = upper[i * owned : (i + 1) * owned, part * pad : (part + 1) * pad]


def shards(voltages):
    samples, channels, local_rows, twice = voltages.shape
    grid_side = twice // 2
    pad_side = 2 * grid_side
    over_ap, over_tm = lax.axis_size("ap"), lax.axis_size("tm")
    own = channels // over_ap
    owned = pad_side // over_tm
    consts = tables(grid_side, pad_side, samples * over_tm)
    vmem = pl.BlockSpec(memory_space=pltpu.VMEM)
    params = pltpu.CompilerParams(vmem_limit_bytes=VMEM_BYTES)
    view = voltages.reshape(samples, channels, local_rows, 2, grid_side)
    view = view.transpose(0, 1, 3, 2, 4).reshape(samples, channels, 2 * local_rows, grid_side)
    order = ORDER if len(ORDER) == channels else tuple(range(channels))
    sent = pl.pallas_call(
        functools.partial(pack, order),
        out_shape=pltpu.VMEM((channels, samples) + view.shape[2:], BF16),
        in_specs=[pl.BlockSpec(memory_space=pltpu.HBM)],
        out_specs=vmem,
        scratch_shapes=[pltpu.VMEM(view.shape, BF16), pltpu.SemaphoreType.DMA((samples,))],
        compiler_params=params,
        name="pack",
    )(pltpu.with_memory_space_constraint(view, pltpu.HBM))
    groups = [
        [(run + channel % own) * over_ap + channel // own for channel in order]
        for run in range(0, over_tm, own)
    ]
    slots = [[order.index(a * own + p) for a in range(over_ap)] for p in range(own)]
    got = lax.all_to_all(sent, ("tm", "ap"), 0, 0, axis_index_groups=groups, tiled=True)
    last = LAST_ORDER if len(LAST_ORDER) == over_tm else tuple(range(over_tm))
    terms = pl.pallas_call(
        functools.partial(correlate, slots, [last.index(t) for t in range(over_tm)]),
        out_shape=jax.ShapeDtypeStruct((over_tm, 2, owned, pad_side), BF16),
        in_specs=[vmem] * (1 + len(consts)),
        out_specs=vmem,
        scratch_shapes=[pltpu.VMEM((pad_side, pad_side), F32)],
        compiler_params=params,
        name="correlate",
    )(got, *[jnp.asarray(c) for c in consts])
    parts = lax.all_to_all(terms, "tm", 0, 0, axis_index_groups=[list(last)], tiled=True)
    sums = [
        sum(parts[i].astype(F32) for i, t in enumerate(last) if t % own == p) for p in range(own)
    ]
    return jnp.stack(sums, 0).transpose(2, 1, 0, 3)


def solution(mesh):
    in_specs = (P("tm", None, "ap", None),)
    out_specs = P("tm", None, "ap", None)
    return jax.shard_map(shards, mesh=mesh, in_specs=in_specs, out_specs=out_specs, check_vma=False)
```

```python
import functools
import math

import jax
import jax.numpy as jnp
import numpy as np
from jax import lax
from jax.experimental import pallas as pl
from jax.experimental.pallas import tpu as pltpu
from jax.sharding import PartitionSpec as P

F32 = jnp.float32
BF16 = jnp.bfloat16
VMEM_BYTES = 48 * 1024 * 1024
ORDER = (
    46, 20, 15, 26, 48, 29, 61, 0, 12, 56, 8, 18, 31, 7, 4, 17,
    43, 54, 23, 53, 57, 28, 16, 36, 51, 62, 1, 41, 63, 13, 50, 10,
    24, 9, 39, 27, 21, 6, 38, 58, 14, 52, 34, 32, 35, 3, 60, 47,
    22, 40, 2, 55, 25, 19, 37, 45, 49, 44, 42, 5, 11, 30, 59, 33,
)
LAST_ORDER = (4, 1, 6, 2, 3, 7, 5, 0)


def angles(rows, cols, pad_side):
    return (rows[:, None] * cols[None, :] % pad_side) * (2.0 * math.pi / pad_side)


def split(table):
    table = table.astype(np.float32)
    high = table.astype(BF16)
    return high, (table - high.astype(np.float32)).astype(BF16)


def tables(grid_side, pad_side, samples):
    dishes, index = np.arange(grid_side), np.arange(pad_side)
    padded = angles(dishes, index, pad_side)
    cosine, sine = np.cos(padded), np.sin(padded)
    first = np.block([[cosine, -sine], [sine, cosine]]).astype(BF16)
    second = np.block([[cosine.T, sine.T], [-sine.T, cosine.T]]).astype(BF16)
    high, low = split(np.concatenate([cosine, sine], 0))
    by_row = np.concatenate([high, high, low], 1)
    whole = angles(index, index, pad_side)
    high, low = split(np.concatenate([np.cos(whole), np.sin(whole)], 1))
    by_col = np.concatenate([high, low, high], 0)
    signed = np.where(index < grid_side, index, index - pad_side)
    pairs = np.maximum(grid_side - np.abs(signed), 0)
    count = pairs[:, None] * pairs[None, :]
    keep = (count > 0) & ((index[:, None] > 0) | (index[None, :] > 0))
    scale = 1.0 / (float(pad_side * pad_side) * np.sqrt(np.maximum(count, 1) * float(samples)))
    factor = np.where(keep, scale, 0.0).astype(np.float32)[:grid_side]
    flip = (dishes[:, None] + dishes[None, :] == grid_side).astype(BF16)
    return first, second, by_row, by_col, factor, flip


def dot(a, b):
    return jnp.dot(a, b, preferred_element_type=F32)


def halves(value):
    high = value.astype(BF16)
    return high, (value - high.astype(F32)).astype(BF16)


def pack(order, x_ref, out_ref, held_ref, sems):
    copies = [
        pltpu.make_async_copy(x_ref.at[t], held_ref.at[t], sems.at[t])
        for t in range(x_ref.shape[0])
    ]
    for copy in copies:
        copy.start()
    for t, copy in enumerate(copies):
        copy.wait()
        for slot, channel in enumerate(order):
            out_ref[slot, t] = held_ref[t, channel]


def rows_of(got_ref, slots, t):
    even = jnp.stack([got_ref[slot, t].astype(F32) for slot in slots[0::2]])
    odd = jnp.stack([got_ref[slot, t].astype(F32) for slot in slots[1::2]])
    count, both, lanes = even.shape
    upper = lax.broadcasted_iota(jnp.int32, even.shape, 1) < both // 2
    real = jnp.where(upper, even, pltpu.roll(odd, both // 2, 1))
    imag = jnp.where(upper, pltpu.roll(even, both // 2, 1), odd)
    rows = count * both
    return jnp.concatenate([real.reshape(rows, lanes), imag.reshape(rows, lanes)], 1).astype(BF16)


def power_of(got_ref, first_ref, second_ref, slots):
    samples = got_ref.shape[1]
    pad = second_ref.shape[1]
    grid_side = pad // 2
    rows = [rows_of(got_ref, slots, t) for t in range(samples)]
    field = dot(jnp.concatenate(rows, 0), first_ref[...]).astype(BF16)
    total = None
    for t in range(samples):
        one = field[t * grid_side : (t + 1) * grid_side]
        beam = dot(second_ref[...], jnp.concatenate([one[:, :pad], one[:, pad:]], 0))
        power = beam[:pad] * beam[:pad] + beam[pad:] * beam[pad:]
        total = power if total is None else total + power
    return total


def correlate(slots, places, got_ref, first_ref, second_ref, by_row, by_col, factor_ref, flip_ref, out_ref, power_ref):
    pad = second_ref.shape[1]
    grid_side = pad // 2
    owned = out_ref.shape[2]
    near = grid_side // owned
    for part, senders in enumerate(slots):
        power = power_of(got_ref, first_ref, second_ref, senders)
        power_ref[...] = power if part == 0 else power_ref[...] + power
    high, low = halves(power_ref[...])
    half = dot(by_row[...], jnp.concatenate([high, low, high], 0))
    high, low = halves(half)
    both = dot(jnp.concatenate([high, high, low], 1), by_col[...])
    cos_cos, cos_sin = both[:grid_side, :pad], both[:grid_side, pad:]
    sin_cos, sin_sin = both[grid_side:, :pad], both[grid_side:, pad:]
    plus = (cos_cos - sin_sin, cos_sin + sin_cos)
    minus = (cos_cos + sin_sin, cos_sin - sin_cos)
    mirrored = [(m * factor_ref[...]).astype(BF16) for m in minus]
    upper = dot(flip_ref[...], jnp.concatenate(mirrored, 1)).astype(BF16)
    for part in range(2):
        lower = (plus[part] * factor_ref[...]).astype(BF16)
        for i in range(near):
            out_ref[places[i], part] = lower[i * owned : (i + 1) * owned]
            out_ref[places[near + i], part] = upper[i * owned : (i + 1) * owned, part * pad : (part + 1) * pad]


def finish(senders, parts_ref, out_ref):
    for p, places in enumerate(senders):
        total = sum(parts_ref[i].astype(F32) for i in places)
        for part in range(2):
            out_ref[:, part, p] = total[part]


def shards(voltages):
    samples, channels, local_rows, twice = voltages.shape
    grid_side = twice // 2
    pad_side = 2 * grid_side
    over_ap, over_tm = lax.axis_size("ap"), lax.axis_size("tm")
    own = channels // over_ap
    owned = pad_side // over_tm
    consts = tables(grid_side, pad_side, samples * over_tm)
    vmem = pl.BlockSpec(memory_space=pltpu.VMEM)
    params = pltpu.CompilerParams(vmem_limit_bytes=VMEM_BYTES)
    view = voltages.reshape(samples, channels, local_rows, 2, grid_side)
    view = view.transpose(0, 1, 3, 2, 4).reshape(samples, channels, 2 * local_rows, grid_side)
    order = ORDER if len(ORDER) == channels else tuple(range(channels))
    sent = pl.pallas_call(
        functools.partial(pack, order),
        out_shape=pltpu.VMEM((channels, samples) + view.shape[2:], BF16),
        in_specs=[pl.BlockSpec(memory_space=pltpu.HBM)],
        out_specs=vmem,
        scratch_shapes=[pltpu.VMEM(view.shape, BF16), pltpu.SemaphoreType.DMA((samples,))],
        compiler_params=params,
        name="pack",
    )(pltpu.with_memory_space_constraint(view, pltpu.HBM))
    groups = [
        [(run + channel % own) * over_ap + channel // own for channel in order]
        for run in range(0, over_tm, own)
    ]
    slots = [[order.index(a * own + p) for a in range(over_ap)] for p in range(own)]
    got = lax.all_to_all(sent, ("tm", "ap"), 0, 0, axis_index_groups=groups, tiled=True)
    last = LAST_ORDER if len(LAST_ORDER) == over_tm else tuple(range(over_tm))
    terms = pl.pallas_call(
        functools.partial(correlate, slots, [last.index(t) for t in range(over_tm)]),
        out_shape=jax.ShapeDtypeStruct((over_tm, 2, owned, pad_side), BF16),
        in_specs=[vmem] * (1 + len(consts)),
        out_specs=vmem,
        scratch_shapes=[pltpu.VMEM((pad_side, pad_side), F32)],
        compiler_params=params,
        name="correlate",
    )(got, *[jnp.asarray(c) for c in consts])
    parts = lax.all_to_all(terms, "tm", 0, 0, axis_index_groups=[list(last)], tiled=True)
    senders = [[i for i, t in enumerate(last) if t % own == p] for p in range(own)]
    return pl.pallas_call(
        functools.partial(finish, senders),
        out_shape=jax.ShapeDtypeStruct((owned, 2, own, pad_side), F32),
        in_specs=[vmem],
        out_specs=vmem,
        compiler_params=params,
        name="finish",
    )(parts)


def solution(mesh):
    in_specs = (P("tm", None, "ap", None),)
    out_specs = P("tm", None, "ap", None)
    return jax.shard_map(shards, mesh=mesh, in_specs=in_specs, out_specs=out_specs, check_vma=False)
```

```python
import functools
import math

import jax
import jax.numpy as jnp
import numpy as np
from jax import lax
from jax.experimental import pallas as pl
from jax.experimental.pallas import tpu as pltpu
from jax.sharding import PartitionSpec as P

F32 = jnp.float32
BF16 = jnp.bfloat16
VMEM_BYTES = 48 * 1024 * 1024
ORDER = (
    46, 20, 15, 26, 48, 29, 61, 0, 12, 56, 8, 18, 31, 7, 4, 17,
    43, 54, 23, 53, 57, 28, 16, 36, 51, 62, 1, 41, 63, 13, 50, 10,
    24, 9, 39, 27, 21, 6, 38, 58, 14, 52, 34, 32, 35, 3, 60, 47,
    22, 40, 2, 55, 25, 19, 37, 45, 49, 44, 42, 5, 11, 30, 59, 33,
)
LAST_ORDER = (4, 1, 6, 2, 3, 7, 5, 0)


def angles(rows, cols, pad_side):
    return (rows[:, None] * cols[None, :] % pad_side) * (2.0 * math.pi / pad_side)


def split(table):
    table = table.astype(np.float32)
    high = table.astype(BF16)
    return high, (table - high.astype(np.float32)).astype(BF16)


def tables(grid_side, pad_side, samples):
    dishes, index = np.arange(grid_side), np.arange(pad_side)
    padded = angles(dishes, index, pad_side)
    cosine, sine = np.cos(padded), np.sin(padded)
    first = np.block([[cosine, -sine], [sine, cosine]]).astype(BF16)
    second = np.block([[cosine.T, sine.T], [-sine.T, cosine.T]]).astype(BF16)
    high, low = split(np.concatenate([cosine, sine], 0))
    by_row = np.concatenate([high, high, low], 1)
    whole = angles(index, index, pad_side)
    high, low = split(np.concatenate([np.cos(whole), np.sin(whole)], 1))
    by_col = np.concatenate([high, low, high], 0)
    signed = np.where(index < grid_side, index, index - pad_side)
    pairs = np.maximum(grid_side - np.abs(signed), 0)
    count = pairs[:, None] * pairs[None, :]
    keep = (count > 0) & ((index[:, None] > 0) | (index[None, :] > 0))
    scale = 1.0 / (float(pad_side * pad_side) * np.sqrt(np.maximum(count, 1) * float(samples)))
    factor = np.where(keep, scale, 0.0).astype(np.float32)[:grid_side]
    flip = (dishes[:, None] + dishes[None, :] == grid_side).astype(BF16)
    return first, second, by_row, by_col, factor, flip


def dot(a, b):
    return jnp.dot(a, b, preferred_element_type=F32)


def halves(value):
    high = value.astype(BF16)
    return high, (value - high.astype(F32)).astype(BF16)


def pack(order, x_ref, out_ref, held_ref, sems):
    chunk = x_ref.shape[0] // sems.shape[0]
    copies = []
    for i in range(sems.shape[0]):
        at = pl.ds(i * chunk, chunk)
        copies.append(pltpu.make_async_copy(x_ref.at[at], held_ref.at[at], sems.at[i]))
    for copy in copies:
        copy.start()
    for i, copy in enumerate(copies):
        copy.wait()
        for t in range(i * chunk, (i + 1) * chunk):
            for slot, channel in enumerate(order):
                out_ref[slot, t] = held_ref[t, channel]


def rows_of(got_ref, slots, t):
    even = jnp.stack([got_ref[slot, t].astype(F32) for slot in slots[0::2]])
    odd = jnp.stack([got_ref[slot, t].astype(F32) for slot in slots[1::2]])
    count, both, lanes = even.shape
    upper = lax.broadcasted_iota(jnp.int32, even.shape, 1) < both // 2
    real = jnp.where(upper, even, pltpu.roll(odd, both // 2, 1))
    imag = jnp.where(upper, pltpu.roll(even, both // 2, 1), odd)
    rows = count * both
    return jnp.concatenate([real.reshape(rows, lanes), imag.reshape(rows, lanes)], 1).astype(BF16)


def power_of(got_ref, first_ref, second_ref, slots):
    samples = got_ref.shape[1]
    pad = second_ref.shape[1]
    grid_side = pad // 2
    rows = [rows_of(got_ref, slots, t) for t in range(samples)]
    field = dot(jnp.concatenate(rows, 0), first_ref[...]).astype(BF16)
    total = None
    for t in range(samples):
        one = field[t * grid_side : (t + 1) * grid_side]
        beam = dot(second_ref[...], jnp.concatenate([one[:, :pad], one[:, pad:]], 0))
        power = beam[:pad] * beam[:pad] + beam[pad:] * beam[pad:]
        total = power if total is None else total + power
    return total


def correlate(slots, places, got_ref, first_ref, second_ref, by_row, by_col, factor_ref, flip_ref, out_ref, power_ref):
    pad = second_ref.shape[1]
    grid_side = pad // 2
    owned = out_ref.shape[2]
    near = grid_side // owned
    for part, senders in enumerate(slots):
        power = power_of(got_ref, first_ref, second_ref, senders)
        power_ref[...] = power if part == 0 else power_ref[...] + power
    high, low = halves(power_ref[...])
    half = dot(by_row[...], jnp.concatenate([high, low, high], 0))
    high, low = halves(half)
    both = dot(jnp.concatenate([high, high, low], 1), by_col[...])
    cos_cos, cos_sin = both[:grid_side, :pad], both[:grid_side, pad:]
    sin_cos, sin_sin = both[grid_side:, :pad], both[grid_side:, pad:]
    plus = (cos_cos - sin_sin, cos_sin + sin_cos)
    minus = (cos_cos + sin_sin, cos_sin - sin_cos)
    mirrored = [(m * factor_ref[...]).astype(BF16) for m in minus]
    upper = dot(flip_ref[...], jnp.concatenate(mirrored, 1)).astype(BF16)
    for part in range(2):
        lower = (plus[part] * factor_ref[...]).astype(BF16)
        for i in range(near):
            out_ref[places[i], part] = lower[i * owned : (i + 1) * owned]
            out_ref[places[near + i], part] = upper[i * owned : (i + 1) * owned, part * pad : (part + 1) * pad]


def finish(senders, parts_ref, out_ref):
    for p, places in enumerate(senders):
        total = sum(parts_ref[i].astype(F32) for i in places)
        for part in range(2):
            out_ref[:, part, p] = total[part]


def shards(voltages):
    samples, channels, local_rows, twice = voltages.shape
    grid_side = twice // 2
    pad_side = 2 * grid_side
    over_ap, over_tm = lax.axis_size("ap"), lax.axis_size("tm")
    own = channels // over_ap
    owned = pad_side // over_tm
    consts = tables(grid_side, pad_side, samples * over_tm)
    vmem = pl.BlockSpec(memory_space=pltpu.VMEM)
    params = pltpu.CompilerParams(vmem_limit_bytes=VMEM_BYTES)
    view = voltages.reshape(samples, channels, local_rows, 2, grid_side)
    view = view.transpose(0, 1, 3, 2, 4).reshape(samples, channels, 2 * local_rows, grid_side)
    order = ORDER if len(ORDER) == channels else tuple(range(channels))
    sent = pl.pallas_call(
        functools.partial(pack, order),
        out_shape=pltpu.VMEM((channels, samples) + view.shape[2:], BF16),
        in_specs=[pl.BlockSpec(memory_space=pltpu.HBM)],
        out_specs=vmem,
        scratch_shapes=[pltpu.VMEM(view.shape, BF16), pltpu.SemaphoreType.DMA((math.gcd(samples, 8),))],
        compiler_params=params,
        name="pack",
    )(pltpu.with_memory_space_constraint(view, pltpu.HBM))
    groups = [
        [(run + channel % own) * over_ap + channel // own for channel in order]
        for run in range(0, over_tm, own)
    ]
    slots = [[order.index(a * own + p) for a in range(over_ap)] for p in range(own)]
    got = lax.all_to_all(sent, ("tm", "ap"), 0, 0, axis_index_groups=groups, tiled=True)
    last = LAST_ORDER if len(LAST_ORDER) == over_tm else tuple(range(over_tm))
    terms = pl.pallas_call(
        functools.partial(correlate, slots, [last.index(t) for t in range(over_tm)]),
        out_shape=jax.ShapeDtypeStruct((over_tm, 2, owned, pad_side), BF16),
        in_specs=[vmem] * (1 + len(consts)),
        out_specs=vmem,
        scratch_shapes=[pltpu.VMEM((pad_side, pad_side), F32)],
        compiler_params=params,
        name="correlate",
    )(got, *[jnp.asarray(c) for c in consts])
    parts = lax.all_to_all(terms, "tm", 0, 0, axis_index_groups=[list(last)], tiled=True)
    senders = [[i for i, t in enumerate(last) if t % own == p] for p in range(own)]
    return pl.pallas_call(
        functools.partial(finish, senders),
        out_shape=jax.ShapeDtypeStruct((owned, 2, own, pad_side), F32),
        in_specs=[vmem],
        out_specs=vmem,
        compiler_params=params,
        name="finish",
    )(parts)


def solution(mesh):
    in_specs = (P("tm", None, "ap", None),)
    out_specs = P("tm", None, "ap", None)
    return jax.shard_map(shards, mesh=mesh, in_specs=in_specs, out_specs=out_specs, check_vma=False)
```

```python
import functools
import math

import jax
import jax.numpy as jnp
import numpy as np
from jax import lax
from jax.experimental import pallas as pl
from jax.experimental.pallas import tpu as pltpu
from jax.sharding import PartitionSpec as P

F32 = jnp.float32
BF16 = jnp.bfloat16
VMEM_BYTES = 48 * 1024 * 1024
ORDER = (
    46, 20, 15, 26, 48, 29, 61, 0, 12, 56, 8, 18, 31, 7, 4, 17,
    43, 54, 23, 53, 57, 28, 16, 36, 51, 62, 1, 41, 63, 13, 50, 10,
    24, 9, 39, 27, 21, 6, 38, 58, 14, 52, 34, 32, 35, 3, 60, 47,
    22, 40, 2, 55, 25, 19, 37, 45, 49, 44, 42, 5, 11, 30, 59, 33,
)
LAST_ORDER = (4, 1, 6, 2, 3, 7, 5, 0)


def angles(rows, cols, pad_side):
    return (rows[:, None] * cols[None, :] % pad_side) * (2.0 * math.pi / pad_side)


def split(table):
    table = table.astype(np.float32)
    high = table.astype(BF16)
    return high, (table - high.astype(np.float32)).astype(BF16)


def tables(grid_side, pad_side, samples):
    dishes, index = np.arange(grid_side), np.arange(pad_side)
    padded = angles(dishes, index, pad_side)
    cosine, sine = np.cos(padded), np.sin(padded)
    first = np.block([[cosine, -sine], [sine, cosine]]).astype(BF16)
    second = np.block([[cosine.T, sine.T], [-sine.T, cosine.T]]).astype(BF16)
    high, low = split(np.concatenate([cosine, sine], 0))
    by_row = np.concatenate([high, high, low], 1)
    whole = angles(index, index, pad_side)
    high, low = split(np.concatenate([np.cos(whole), np.sin(whole)], 1))
    by_col = np.concatenate([high, low, high], 0)
    signed = np.where(index < grid_side, index, index - pad_side)
    pairs = np.maximum(grid_side - np.abs(signed), 0)
    count = pairs[:, None] * pairs[None, :]
    keep = (count > 0) & ((index[:, None] > 0) | (index[None, :] > 0))
    scale = 1.0 / (float(pad_side * pad_side) * np.sqrt(np.maximum(count, 1) * float(samples)))
    factor = np.where(keep, scale, 0.0).astype(np.float32)[:grid_side]
    flip = (dishes[:, None] + dishes[None, :] == grid_side).astype(BF16)
    return first, second, by_row, by_col, factor, flip


def dot(a, b):
    return jnp.dot(a, b, preferred_element_type=F32)


def halves(value):
    high = value.astype(BF16)
    return high, (value - high.astype(F32)).astype(BF16)


def pack(order, x_ref, out_ref, held_ref, sems):
    chunk = x_ref.shape[0] // sems.shape[0]
    copies = []
    for i in range(sems.shape[0]):
        at = pl.ds(i * chunk, chunk)
        copies.append(pltpu.make_async_copy(x_ref.at[at], held_ref.at[at], sems.at[i]))
    for copy in copies:
        copy.start()
    for i, copy in enumerate(copies):
        copy.wait()
        for t in range(i * chunk, (i + 1) * chunk):
            for slot, channel in enumerate(order):
                out_ref[slot, t] = held_ref[t, channel]


def rows_of(got_ref, slots, t):
    even = jnp.stack([got_ref[slot, t].astype(F32) for slot in slots[0::2]])
    odd = jnp.stack([got_ref[slot, t].astype(F32) for slot in slots[1::2]])
    count, both, lanes = even.shape
    upper = lax.broadcasted_iota(jnp.int32, even.shape, 1) < both // 2
    real = jnp.where(upper, even, pltpu.roll(odd, both // 2, 1))
    imag = jnp.where(upper, pltpu.roll(even, both // 2, 1), odd)
    rows = count * both
    return jnp.concatenate([real.reshape(rows, lanes), imag.reshape(rows, lanes)], 1).astype(BF16)


def power_of(got_ref, first_ref, second_ref, slots):
    samples = got_ref.shape[1]
    pad = second_ref.shape[1]
    grid_side = pad // 2
    rows = [rows_of(got_ref, slots, t) for t in range(samples)]
    field = dot(jnp.concatenate(rows, 0), first_ref[...]).astype(BF16)
    total = None
    for t in range(samples):
        one = field[t * grid_side : (t + 1) * grid_side]
        beam = dot(second_ref[...], jnp.concatenate([one[:, :pad], one[:, pad:]], 0))
        power = beam[:pad] * beam[:pad] + beam[pad:] * beam[pad:]
        total = power if total is None else total + power
    return total


def correlate(slots, places, got_ref, first_ref, second_ref, by_row, by_col, factor_ref, flip_ref, out_ref, power_ref):
    pad = second_ref.shape[1]
    grid_side = pad // 2
    owned = out_ref.shape[2]
    near = grid_side // owned
    for part, senders in enumerate(slots):
        power = power_of(got_ref, first_ref, second_ref, senders)
        power_ref[...] = power if part == 0 else power_ref[...] + power
    high, low = halves(power_ref[...])
    half = dot(by_row[...], jnp.concatenate([high, low, high], 0))
    high, low = halves(half)
    both = dot(jnp.concatenate([high, high, low], 1), by_col[...])
    cos_cos, cos_sin = both[:grid_side, :pad], both[:grid_side, pad:]
    sin_cos, sin_sin = both[grid_side:, :pad], both[grid_side:, pad:]
    plus = (cos_cos - sin_sin, cos_sin + sin_cos)
    minus = (cos_cos + sin_sin, cos_sin - sin_cos)
    mirrored = [(m * factor_ref[...]).astype(BF16) for m in minus]
    upper = dot(flip_ref[...], jnp.concatenate(mirrored, 1)).astype(BF16)
    for part in range(2):
        lower = (plus[part] * factor_ref[...]).astype(BF16)
        for i in range(near):
            out_ref[places[i], part] = lower[i * owned : (i + 1) * owned]
            out_ref[places[near + i], part] = upper[i * owned : (i + 1) * owned, part * pad : (part + 1) * pad]


def finish(senders, parts_ref, out_ref):
    for p, places in enumerate(senders):
        total = sum(parts_ref[i].astype(F32) for i in places)
        for part in range(2):
            out_ref[:, part, p] = total[part]


def shards(voltages):
    samples, channels, local_rows, twice = voltages.shape
    grid_side = twice // 2
    pad_side = 2 * grid_side
    over_ap, over_tm = lax.axis_size("ap"), lax.axis_size("tm")
    own = channels // over_ap
    owned = pad_side // over_tm
    consts = tables(grid_side, pad_side, samples * over_tm)
    vmem = pl.BlockSpec(memory_space=pltpu.VMEM)
    params = pltpu.CompilerParams(vmem_limit_bytes=VMEM_BYTES)
    view = voltages.reshape(samples, channels, local_rows, 2, grid_side)
    view = view.transpose(0, 1, 3, 2, 4).reshape(samples, channels, 2 * local_rows, grid_side)
    order = ORDER if len(ORDER) == channels else tuple(range(channels))
    sent = pl.pallas_call(
        functools.partial(pack, order),
        out_shape=pltpu.VMEM((channels, samples) + view.shape[2:], BF16),
        in_specs=[pl.BlockSpec(memory_space=pltpu.HBM)],
        out_specs=vmem,
        scratch_shapes=[pltpu.VMEM(view.shape, BF16), pltpu.SemaphoreType.DMA((math.gcd(samples, 4),))],
        compiler_params=params,
        name="pack",
    )(pltpu.with_memory_space_constraint(view, pltpu.HBM))
    groups = [
        [(run + channel % own) * over_ap + channel // own for channel in order]
        for run in range(0, over_tm, own)
    ]
    slots = [[order.index(a * own + p) for a in range(over_ap)] for p in range(own)]
    got = lax.all_to_all(sent, ("tm", "ap"), 0, 0, axis_index_groups=groups, tiled=True)
    last = LAST_ORDER if len(LAST_ORDER) == over_tm else tuple(range(over_tm))
    terms = pl.pallas_call(
        functools.partial(correlate, slots, [last.index(t) for t in range(over_tm)]),
        out_shape=jax.ShapeDtypeStruct((over_tm, 2, owned, pad_side), BF16),
        in_specs=[vmem] * (1 + len(consts)),
        out_specs=vmem,
        scratch_shapes=[pltpu.VMEM((pad_side, pad_side), F32)],
        compiler_params=params,
        name="correlate",
    )(got, *[jnp.asarray(c) for c in consts])
    parts = lax.all_to_all(terms, "tm", 0, 0, axis_index_groups=[list(last)], tiled=True)
    senders = [[i for i, t in enumerate(last) if t % own == p] for p in range(own)]
    return pl.pallas_call(
        functools.partial(finish, senders),
        out_shape=jax.ShapeDtypeStruct((owned, 2, own, pad_side), F32),
        in_specs=[vmem],
        out_specs=vmem,
        compiler_params=params,
        name="finish",
    )(parts)


def solution(mesh):
    in_specs = (P("tm", None, "ap", None),)
    out_specs = P("tm", None, "ap", None)
    return jax.shard_map(shards, mesh=mesh, in_specs=in_specs, out_specs=out_specs, check_vma=False)
```

```python
import functools
import math

import jax
import jax.numpy as jnp
import numpy as np
from jax import lax
from jax.experimental import pallas as pl
from jax.experimental.pallas import tpu as pltpu
from jax.sharding import PartitionSpec as P

F32 = jnp.float32
BF16 = jnp.bfloat16
VMEM_BYTES = 48 * 1024 * 1024
ORDER = (
    46, 20, 15, 26, 48, 29, 61, 0, 12, 56, 8, 18, 31, 7, 4, 17,
    43, 54, 23, 53, 57, 28, 16, 36, 51, 62, 1, 41, 63, 13, 50, 10,
    24, 9, 39, 27, 21, 6, 38, 58, 14, 52, 34, 32, 35, 3, 60, 47,
    22, 40, 2, 55, 25, 19, 37, 45, 49, 44, 42, 5, 11, 30, 59, 33,
)
LAST_ORDER = (4, 1, 6, 2, 3, 7, 5, 0)


def angles(rows, cols, pad_side):
    return (rows[:, None] * cols[None, :] % pad_side) * (2.0 * math.pi / pad_side)


def split(table):
    table = table.astype(np.float32)
    high = table.astype(BF16)
    return high, (table - high.astype(np.float32)).astype(BF16)


def tables(grid_side, pad_side, samples):
    dishes, index = np.arange(grid_side), np.arange(pad_side)
    padded = angles(dishes, index, pad_side)
    cosine, sine = np.cos(padded), np.sin(padded)
    first = np.block([[cosine, -sine], [sine, cosine]]).astype(BF16)
    second = np.block([[cosine.T, sine.T], [-sine.T, cosine.T]]).astype(BF16)
    high, low = split(np.concatenate([cosine, sine], 0))
    by_row = np.concatenate([high, high, low], 1)
    whole = angles(index, index, pad_side)
    high, low = split(np.concatenate([np.cos(whole), np.sin(whole)], 1))
    by_col = np.concatenate([high, low, high], 0)
    signed = np.where(index < grid_side, index, index - pad_side)
    pairs = np.maximum(grid_side - np.abs(signed), 0)
    count = pairs[:, None] * pairs[None, :]
    keep = (count > 0) & ((index[:, None] > 0) | (index[None, :] > 0))
    scale = 1.0 / (float(pad_side * pad_side) * np.sqrt(np.maximum(count, 1) * float(samples)))
    factor = np.where(keep, scale, 0.0).astype(np.float32)[:grid_side]
    flip = (dishes[:, None] + dishes[None, :] == grid_side).astype(BF16)
    return first, second, by_row, by_col, factor, flip


def dot(a, b):
    return jnp.dot(a, b, preferred_element_type=F32)


def halves(value):
    high = value.astype(BF16)
    return high, (value - high.astype(F32)).astype(BF16)


def pack(order, x_ref, out_ref, held_ref, sems):
    chunk = x_ref.shape[0] // sems.shape[0]
    copies = []
    for i in range(sems.shape[0]):
        at = pl.ds(i * chunk, chunk)
        copies.append(pltpu.make_async_copy(x_ref.at[at], held_ref.at[at], sems.at[i]))
    for copy in copies:
        copy.start()
    for i, copy in enumerate(copies):
        copy.wait()
        for t in range(i * chunk, (i + 1) * chunk):
            for slot, channel in enumerate(order):
                out_ref[slot, t] = held_ref[t, channel]


def rows_of(got_ref, slots, t):
    even = jnp.stack([got_ref[slot, t].astype(F32) for slot in slots[0::2]])
    odd = jnp.stack([got_ref[slot, t].astype(F32) for slot in slots[1::2]])
    count, both, lanes = even.shape
    upper = lax.broadcasted_iota(jnp.int32, even.shape, 1) < both // 2
    real = jnp.where(upper, even, pltpu.roll(odd, both // 2, 1))
    imag = jnp.where(upper, pltpu.roll(even, both // 2, 1), odd)
    rows = count * both
    return jnp.concatenate([real.reshape(rows, lanes), imag.reshape(rows, lanes)], 1).astype(BF16)


def power_of(got_ref, first_ref, second_ref, slots):
    samples = got_ref.shape[1]
    pad = second_ref.shape[1]
    grid_side = pad // 2
    rows = [rows_of(got_ref, senders, t) for senders in slots for t in range(samples)]
    field = dot(jnp.concatenate(rows, 0), first_ref[...]).astype(BF16)
    total = None
    for t in range(len(rows)):
        one = field[t * grid_side : (t + 1) * grid_side]
        beam = dot(second_ref[...], jnp.concatenate([one[:, :pad], one[:, pad:]], 0))
        power = beam[:pad] * beam[:pad] + beam[pad:] * beam[pad:]
        total = power if total is None else total + power
    return total


def correlate(slots, places, got_ref, first_ref, second_ref, by_row, by_col, factor_ref, flip_ref, out_ref, power_ref):
    pad = second_ref.shape[1]
    grid_side = pad // 2
    owned = out_ref.shape[2]
    near = grid_side // owned
    power_ref[...] = power_of(got_ref, first_ref, second_ref, slots)
    high, low = halves(power_ref[...])
    half = dot(by_row[...], jnp.concatenate([high, low, high], 0))
    high, low = halves(half)
    both = dot(jnp.concatenate([high, high, low], 1), by_col[...])
    cos_cos, cos_sin = both[:grid_side, :pad], both[:grid_side, pad:]
    sin_cos, sin_sin = both[grid_side:, :pad], both[grid_side:, pad:]
    plus = (cos_cos - sin_sin, cos_sin + sin_cos)
    minus = (cos_cos + sin_sin, cos_sin - sin_cos)
    mirrored = [(m * factor_ref[...]).astype(BF16) for m in minus]
    upper = dot(flip_ref[...], jnp.concatenate(mirrored, 1)).astype(BF16)
    for part in range(2):
        lower = (plus[part] * factor_ref[...]).astype(BF16)
        for i in range(near):
            out_ref[places[i], part] = lower[i * owned : (i + 1) * owned]
            out_ref[places[near + i], part] = upper[i * owned : (i + 1) * owned, part * pad : (part + 1) * pad]


def finish(senders, parts_ref, out_ref):
    for p, places in enumerate(senders):
        total = sum(parts_ref[i].astype(F32) for i in places)
        for part in range(2):
            out_ref[:, part, p] = total[part]


def shards(voltages):
    samples, channels, local_rows, twice = voltages.shape
    grid_side = twice // 2
    pad_side = 2 * grid_side
    over_ap, over_tm = lax.axis_size("ap"), lax.axis_size("tm")
    own = channels // over_ap
    owned = pad_side // over_tm
    consts = tables(grid_side, pad_side, samples * over_tm)
    vmem = pl.BlockSpec(memory_space=pltpu.VMEM)
    params = pltpu.CompilerParams(vmem_limit_bytes=VMEM_BYTES)
    view = voltages.reshape(samples, channels, local_rows, 2, grid_side)
    view = view.transpose(0, 1, 3, 2, 4).reshape(samples, channels, 2 * local_rows, grid_side)
    order = ORDER if len(ORDER) == channels else tuple(range(channels))
    sent = pl.pallas_call(
        functools.partial(pack, order),
        out_shape=pltpu.VMEM((channels, samples) + view.shape[2:], BF16),
        in_specs=[pl.BlockSpec(memory_space=pltpu.HBM)],
        out_specs=vmem,
        scratch_shapes=[pltpu.VMEM(view.shape, BF16), pltpu.SemaphoreType.DMA((math.gcd(samples, 4),))],
        compiler_params=params,
        name="pack",
    )(pltpu.with_memory_space_constraint(view, pltpu.HBM))
    groups = [
        [(run + channel % own) * over_ap + channel // own for channel in order]
        for run in range(0, over_tm, own)
    ]
    slots = [[order.index(a * own + p) for a in range(over_ap)] for p in range(own)]
    got = lax.all_to_all(sent, ("tm", "ap"), 0, 0, axis_index_groups=groups, tiled=True)
    last = LAST_ORDER if len(LAST_ORDER) == over_tm else tuple(range(over_tm))
    terms = pl.pallas_call(
        functools.partial(correlate, slots, [last.index(t) for t in range(over_tm)]),
        out_shape=jax.ShapeDtypeStruct((over_tm, 2, owned, pad_side), BF16),
        in_specs=[vmem] * (1 + len(consts)),
        out_specs=vmem,
        scratch_shapes=[pltpu.VMEM((pad_side, pad_side), F32)],
        compiler_params=params,
        name="correlate",
    )(got, *[jnp.asarray(c) for c in consts])
    parts = lax.all_to_all(terms, "tm", 0, 0, axis_index_groups=[list(last)], tiled=True)
    senders = [[i for i, t in enumerate(last) if t % own == p] for p in range(own)]
    return pl.pallas_call(
        functools.partial(finish, senders),
        out_shape=jax.ShapeDtypeStruct((owned, 2, own, pad_side), F32),
        in_specs=[vmem],
        out_specs=vmem,
        compiler_params=params,
        name="finish",
    )(parts)


def solution(mesh):
    in_specs = (P("tm", None, "ap", None),)
    out_specs = P("tm", None, "ap", None)
    return jax.shard_map(shards, mesh=mesh, in_specs=in_specs, out_specs=out_specs, check_vma=False)
```
